256 devices in a mesh: col: 32 (over z, y), row: 8 (over x, core).
Axes of the slice: x: 4, y: 4, z: 8, core: 2. Of those that a mesh axis runs over, the one named last changes fastest.
Arguments:
- slab: float32 [48, 8, 128, 2, 32, 128], P(None, 'row', None, None, 'col'), may hold values from 0 to 1.4, as said below
Outputs:
- updated: float32 [48, 8, 128, 2, 32, 128], P(None, 'row', None, None, 'col')
The draws below stay inside these ranges and needn't reach their ends.
Inputs may be any that keep to these rules, and one draw needn't show every extreme that they name: `slab`: entry [g, h] is exp(-sum over the 256 features of a positive rate times the squared difference of the two designs' features), plus a noise variance of 0.1 to 0.4 where g equals h; the leading 8192 x 8192 part is symmetric positive definite.
All inputs are finite; a program needn't handle non-finite values.
Results may differ from the reference program's by a relative error of at most 0.0003.
Values sent between devices are 32-bit elements; how exact they have to be, the bound alone decides.
No kernel may reach another device: no remote copies, remote signals or barrier semaphores. Data moves between devices by JAX's collectives and lax.ppermute only.
A program may use at most 128 MiB of HBM per device.

```python
import jax
import jax.numpy as jnp
from jax import lax

NB = 128
FEAT = 256
RB_DEV = 48
CB_DEV = 2
ORDER = 49152
SLAB = 8192
N_COL = 32
N_ROW = 8


def draw_slab(key, part):
    key = jax.random.fold_in(key, 11)
    first, second, third = jax.random.split(key, 3)
    rates = 2.25 * jnp.exp(-(FEAT / 4.0) * jax.random.uniform(second, (FEAT,), jnp.float32))
    designs = jax.random.uniform(first, (ORDER, FEAT), jnp.float32)
    noise = 0.1 * jnp.exp(jax.random.uniform(third, (SLAB,), jnp.float32, 0.0, 1.3862))
    scaled = designs * jnp.sqrt(rates)[None, :]
    columns = scaled[:SLAB]

    def kernel_rows(group):
        diff = group[:, None, :] - columns[None, :, :]
        return jnp.exp(-jnp.sum(diff * diff, axis=2))
    kernel = lax.map(kernel_rows, scaled.reshape(ORDER // 8, 8, FEAT)).reshape(ORDER, SLAB)
    index = jnp.arange(SLAB)
    kernel = kernel.at[index, index].add(noise)
    return kernel.reshape(RB_DEV, N_ROW, NB, CB_DEV, N_COL, NB)


def setup_inputs(seed: int = 0) -> dict:
    streams_of = jax.random.split(jax.random.key(seed), 2)
    slab = draw_slab(jax.random.fold_in(streams_of[1], 71), 0)
    return dict(slab=slab)


def reference(slab):
    whole = slab.reshape(ORDER, SLAB)
    rows = jnp.arange(ORDER)
    for step in range(2):
        low, high = (step * NB, (step + 1) * NB)
        factor = jnp.linalg.cholesky(whole[low:high, low:high])
        solved = lax.linalg.triangular_solve(factor, whole[:, low:high], left_side=False, lower=True, transpose_a=True)
        below = (rows >= high)[:, None]
        lowpart = jnp.where(below, solved, 0.0)
        columns = lowpart[:SLAB]

        def update(pair):
            block, left = pair
            return block - jnp.dot(left.astype(jnp.float32), columns.T.astype(jnp.float32), precision=lax.Precision.HIGHEST, preferred_element_type=jnp.float32)
        blocks = lax.map(update, (whole.reshape(ORDER // NB, NB, SLAB), lowpart.reshape(ORDER // NB, NB, NB)))
        whole = blocks.reshape(ORDER, SLAB)
        inside = ((rows >= low) & (rows < high))[:, None]
        panel = jnp.where(below, solved, jnp.where(inside, jnp.tile(factor, (ORDER // NB, 1)), 0.0))
        whole = whole.at[:, low:high].set(panel)
    return whole.reshape(slab.shape)
```

```python
import functools

import jax
import jax.numpy as jnp
import numpy as np
from jax import lax
from jax.experimental import pallas as pl
from jax.experimental.pallas import tpu as pltpu
from jax.sharding import PartitionSpec as P

F32 = jnp.float32
BF16 = jnp.bfloat16
NZ, NY = 8, 4
ROOTS = (0, 1)
SUBROOTS = ((0, 1), (0, 3), (3, 0), (5, 0))
QUARTERS = [(0, 1), (2, 1), (2, 2), (3, 1), (0, 3), (1, 3), (2, 0), (3, 3), (0, 0), (1, 0), (1, 1), (3, 0), (0, 2), (1, 2), (2, 3), (3, 2)]
DELIVER = [
    [(0, 4, 1, 1), (1, 9, 1, 0), (2, 11, 2, 1), (3, 15, 3, 0), (12, 18, 0, 0), (13, 31, 3, 1), (20, 25, 2, 0), (21, 17, 0, 1)],
    [(0, 18, 0, 1), (1, 13, 3, 0), (2, 10, 1, 1), (3, 26, 2, 0), (12, 5, 2, 0), (13, 6, 2, 1), (20, 28, 3, 0), (21, 8, 2, 1)],
    [(0, 9, 2, 1), (1, 31, 3, 0), (2, 24, 1, 1), (3, 29, 3, 0), (12, 4, 1, 0), (13, 23, 1, 1), (20, 14, 3, 0), (21, 7, 1, 1)],
    [(0, 22, 1, 1), (1, 19, 0, 0), (2, 16, 0, 1), (3, 17, 0, 0), (12, 23, 2, 0), (13, 5, 1, 1), (20, 2, 0, 0), (21, 29, 3, 1)],
    [(0, 12, 3, 1), (1, 27, 1, 0), (2, 25, 2, 1), (3, 7, 1, 0), (12, 22, 1, 0), (13, 20, 2, 1), (20, 6, 1, 0), (21, 3, 0, 1)],
    [(0, 30, 3, 1), (1, 24, 2, 0), (2, 28, 3, 1), (3, 8, 2, 0), (13, 19, 0, 1), (20, 11, 2, 0), (21, 15, 3, 1)],
    [(0, 27, 2, 1), (1, 10, 2, 0), (2, 14, 3, 1), (3, 21, 1, 0), (12, 30, 3, 0), (20, 16, 0, 0), (21, 26, 2, 1)],
]
GATHER = (
    ((1, 0), (0, 0), 0), ((-1, 0), (0, 0), 0), ((0, 1), (0, 0), 0), ((0, -1), (0, 0), 0),
    ((1, 0), (1, 0), 0), ((-1, 0), (-1, 0), 0), ((0, 1), (1, 0), 0), ((0, -1), (1, 0), 0),
    ((0, 1), (-1, 0), 0), ((0, -1), (-1, 0), 0), ((1, 0), (2, 0), 0), ((-1, 0), (-2, 0), 0),
    ((0, 1), (0, 1), 1), ((0, -1), (0, -1), 2), ((1, 0), (1, 1), 0), ((-1, 0), (-1, 1), 0),
)


def at(z, y):
    return (z % NZ) * NY + y % NY


def place(chip):
    return chip // NY, chip % NY


CLASSES = []
for _z in range(NZ):
    for _y in range(NY):
        if not any((_z, _y) in _c for _c in CLASSES):
            CLASSES.append(((_z, _y), ((_z + 4) % NZ, (_y + 2) % NY)))
CLASS_OF = {at(*_m): _i for _i, _c in enumerate(CLASSES) for _m in _c}
PIECES = len(CLASSES)
CHIPS = NZ * NY


def tables():
    order = np.zeros((CHIPS, PIECES), np.int32)
    for chip in range(CHIPS):
        shift = 1 if chip == ROOTS[1] else 0
        order[chip] = [CLASS_OF[at(z, y + shift)] for z, y in QUARTERS]
    origin = np.zeros((2, CHIPS), np.int32)
    index = np.zeros((len(DELIVER), CHIPS), np.int32)
    for step, sends in enumerate(DELIVER):
        for source, target, slot, panel in sends:
            origin[panel, target] = step
            index[step, source] = slot
    held = np.zeros(CHIPS, np.int32)
    for quarter, (z, y) in enumerate(SUBROOTS):
        first = [CLASS_OF[at(*m)] for m in QUARTERS[4 * quarter : 4 * quarter + 4]]
        for panel in (0, 1):
            chip = at(z, y + panel)
            held[chip] = first.index(CLASS_OF[at(z, y)])
            origin[panel, chip] = len(DELIVER)
    for panel in (0, 1):
        origin[panel, ROOTS[panel]] = len(DELIVER) + 1
    mine = [CLASS_OF[at(*m)] for m in QUARTERS].index(CLASS_OF[at(0, 0)])
    return order, origin, index, held, mine


ORDER, ORIGIN, INDEX, HELD, MINE = tables()


def extract_kernel(rows, order_ref, x_ref, o_ref):
    o_ref[0] = x_ref[pl.ds(0, rows, stride=2), :]


def extract(x, order, rows):
    return pl.pallas_call(
        functools.partial(extract_kernel, rows),
        grid_spec=pltpu.PrefetchScalarGridSpec(
            num_scalar_prefetch=1,
            grid=(PIECES,),
            in_specs=[pl.BlockSpec((2 * rows, 128), lambda i, order: (order[i], 0))],
            out_specs=pl.BlockSpec((1, rows, 128), lambda i, order: (i, 0, 0)),
        ),
        out_shape=jax.ShapeDtypeStruct((PIECES, rows, 128), F32),
    )(order, x)


class Sender:
    def __init__(self, depth):
        self.depth = depth
        self.sent = []

    def __call__(self, value, pairs):
        if len(self.sent) >= self.depth:
            oldest = self.sent[-self.depth]
            value, oldest[0] = lax.optimization_barrier((value, oldest[0]))
        result = [lax.ppermute(value, "col", pairs)]
        self.sent.append(result)
        return result


def spread(own, chip):
    send = Sender(5)
    quarters = [
        send(own[4 * k : 4 * k + 4], [(at(0, p), at(z, y + p)) for p in (0, 1)])
        for k, (z, y) in enumerate(SUBROOTS)
    ]
    quarter = sum(q[0] for q in quarters)
    index = jnp.asarray(INDEX)[:, chip]
    arrived = [
        send(
            lax.dynamic_index_in_dim(quarter, index[step], 0, keepdims=False),
            [(source, target) for source, target, _, _ in sends],
        )
        for step, sends in enumerate(DELIVER)
    ]
    held = lax.dynamic_index_in_dim(quarter, jnp.asarray(HELD)[chip], 0, keepdims=False)
    choices = [a[0] for a in arrived] + [held, own[MINE]]

    def pick(panel):
        origin = jnp.asarray(ORIGIN)[panel, chip]
        value = choices[0]
        for k in range(1, len(choices)):
            value = jnp.where(origin == k, choices[k], value)
        return value

    pieces = {(0, 0): [jnp.stack([pick(0), pick(1)])]}
    for (fz, fy), (ez, ey), half in GATHER:
        value = pieces[(ez, ey)][0]
        middle = value.shape[1] // 2
        value = {0: value, 1: value[:, :middle], 2: value[:, middle:]}[half]
        pairs = [(at(z + fz, y + fy), at(z, y)) for z in range(NZ) for y in range(NY)]
        key = (fz + ez, fy + ey) if half == 0 else (0, 2, half)
        pieces[key] = send(value, pairs)
    return {key: value[0] for key, value in pieces.items()}


def corner(head, chip):
    z, y = chip // NY, chip % NY
    move = lambda value, pairs: lax.ppermute(value, "col", pairs)
    up = move(head, [(0, 1), (1, 2)])
    down = move(head, [(0, 3), (1, 0)])
    across = move(head, [(0, 2), (1, 3)])
    first = jnp.where(y == 0, head, jnp.where(y == 1, up, jnp.where(y == 2, across, down)))
    second = jnp.where(y == 1, head, jnp.where(y == 2, up, jnp.where(y == 3, across, down)))
    line = jnp.concatenate([first, second], axis=1)
    far = move(line, [(at(0, j), at(3, j)) for j in range(NY)])
    back = move(line, [(at(0, j), at(5, j)) for j in range(NY)])
    base = jnp.where(z == 0, line, jnp.where(z == 3, far, back))
    above = move(base, [(at(k, j), at(k + 1, j)) for k in (0, 3, 5) for j in range(NY)])
    below = move(base, [(at(k, j), at(k - 1, j)) for k in (0, 3) for j in range(NY)])
    near = (z == 0) | (z == 3) | (z == 5)
    return jnp.where(near, base, jnp.where((z == 1) | (z == 4) | (z == 6), above, below))


def dot(a, b, dims):
    return lax.dot_general(
        a, b, ((dims[:1], dims[1:]), ((), ())), precision=lax.Precision.HIGHEST, preferred_element_type=F32
    )


def eliminate(block):
    n = block.shape[0]
    block = 0.5 * (block + block.T)
    row_id = lax.broadcasted_iota(jnp.int32, (8, n), 0)
    lane_id = lax.broadcasted_iota(jnp.int32, (8, n), 1)
    left = [block[8 * k : 8 * k + 8] for k in range(n // 8)]
    right = [jnp.where(lane_id == row_id + 8 * k, 1.0, 0.0).astype(F32) for k in range(n // 8)]
    for j in range(n):
        k0, r = j // 8, j % 8
        pivot = jnp.broadcast_to(left[k0][r : r + 1, j : j + 1], (8, n))
        scale = lax.rsqrt(pivot)
        scale = scale * (1.5 - 0.5 * pivot * scale * scale)
        lrow = jnp.broadcast_to(left[k0][r : r + 1, :], (8, n)) * scale
        rrow = jnp.broadcast_to(right[k0][r : r + 1, :], (8, n)) * scale
        for k in range(k0, n // 8):
            factor = jnp.broadcast_to(left[k][:, j : j + 1], (8, n)) * scale
            if k == k0:
                below = row_id > r
                left[k] = jnp.where(below, left[k] - factor * lrow, jnp.where(row_id == r, lrow, left[k]))
                right[k] = jnp.where(below, right[k] - factor * rrow, jnp.where(row_id == r, rrow, right[k]))
            else:
                left[k] = left[k] - factor * lrow
                right[k] = right[k] - factor * rrow
    upper = jnp.concatenate(left, axis=0)
    rows = lax.broadcasted_iota(jnp.int32, (n, n), 0)
    lanes = lax.broadcasted_iota(jnp.int32, (n, n), 1)
    return jnp.where(lanes >= rows, upper, 0.0), jnp.concatenate(right, axis=0)


def first_kernel(a_ref, d_ref, w_ref):
    upper, inverse = eliminate(a_ref[...])
    d_ref[...] = upper.T
    w_ref[...] = inverse


def second_kernel(a10_ref, a11_ref, w0_ref, l_ref, d_ref, w_ref):
    low = dot(a10_ref[...], w0_ref[...], (1, 1))
    l_ref[...] = low
    upper, inverse = eliminate(a11_ref[...] - dot(low, low, (1, 1)))
    d_ref[...] = upper.T
    w_ref[...] = inverse


def third_kernel(place_ref, head_ref, d0_ref, w0_ref, l_ref, d1_ref, w1_ref, m_ref, s_ref):
    row, col = place_ref[0], place_ref[1]
    w0, w1, low = w0_ref[...], w1_ref[...], l_ref[...]
    head0, head1 = head_ref[:128], head_ref[128:]
    g0 = dot(w0, head0, (1, 0))
    rest = head1 - dot(low, g0, (1, 0))
    g1 = dot(w1, rest, (1, 0))
    m1 = dot(w1, g1, (0, 0))
    m0 = dot(w0, g0 - dot(low, m1, (0, 0)), (0, 0))
    mixed = dot(w0, dot(low, w1, (0, 1)), (0, 0))
    zero = jnp.zeros((128, 128), F32)
    root0, root1 = col == ROOTS[0], col == ROOTS[1]
    m_ref[:128, 128:] = m0[:, 128:]
    m_ref[128:, 128:] = m1[:, 128:]
    m_ref[:128, :128] = jnp.where(root0, -w0.T, jnp.where(root1, mixed, m0[:, :128]))
    m_ref[128:, :128] = jnp.where(root0, zero, jnp.where(root1, -w1.T, m1[:, :128]))
    top = row == 0
    s_ref[:, 128:] = jnp.where(top, head0[:, 128:], rest[:, 128:])
    normal = jnp.where(top, head0[:, :128], rest[:, :128])
    on0 = jnp.where(top, d0_ref[...], low)
    on1 = jnp.where(top, zero, d1_ref[...])
    s_ref[:, :128] = jnp.where(root0, on0, jnp.where(root1, on1, normal))


def vmem(count):
    return [pl.BlockSpec(memory_space=pltpu.VMEM)] * count


def factor_all(corner_block, head, row, col):
    square = jax.ShapeDtypeStruct((128, 128), F32)
    d0, w0 = pl.pallas_call(
        first_kernel, out_shape=(square, square), in_specs=vmem(1), out_specs=tuple(vmem(2))
    )(corner_block[:128, :128])
    low, d1, w1 = pl.pallas_call(
        second_kernel, out_shape=(square,) * 3, in_specs=vmem(3), out_specs=tuple(vmem(3))
    )(corner_block[128:, :128], corner_block[128:, 128:], w0)
    return pl.pallas_call(
        third_kernel,
        out_shape=(jax.ShapeDtypeStruct((256, 256), F32), jax.ShapeDtypeStruct((128, 256), F32)),
        in_specs=[pl.BlockSpec(memory_space=pltpu.SMEM)] + vmem(6),
        out_specs=tuple(vmem(2)),
    )(jnp.stack([row, col]).astype(jnp.int32), head, d0, w0, low, d1, w1)


def update_kernel(names, rows, chunk_ref, place_ref, x_ref, m_ref, s_ref, *refs):
    pieces, o_ref, wide = refs[: sum(len(n) for n in names)], refs[-2], refs[-1]
    step = pl.program_id(0)
    k = 0
    for i, parts in enumerate(names):
        mine = pieces[k : k + len(parts)]
        k += len(parts)

        @pl.when(step == i)
        def _():
            start = 0
            for ref in mine:
                size = ref.shape[1]
                wide[start : start + size, :128] = ref[0]
                wide[start : start + size, 128:] = ref[1]
                start += size

    value = wide[...]
    high = value.astype(BF16)
    rest = (value - high.astype(F32)).astype(BF16)
    m = m_ref[...]
    m_high = m.astype(BF16)
    m_rest = (m - m_high.astype(F32)).astype(BF16)
    mul = functools.partial(jnp.dot, preferred_element_type=F32)
    product = mul(high, m_high) + (mul(rest, m_high) + mul(high, m_rest))
    root = place_ref[1] < 2
    left = x_ref[pl.ds(0, rows, stride=2), :]
    o_ref[pl.ds(0, rows, stride=2), :] = jnp.where(root, 0.0, left) - product[:, :128]
    o_ref[pl.ds(1, rows, stride=2), :] = x_ref[pl.ds(1, rows, stride=2), :] - product[:, 128:]

    @pl.when((chunk_ref[step] == 0) & (place_ref[0] < 2))
    def _():
        o_ref[pl.ds(0, 128, stride=2), :] = s_ref[:, :128]
        o_ref[pl.ds(1, 128, stride=2), :] = s_ref[:, 128:]


def update(x, m, special, pieces, chunks, row, col, names, rows):
    block = pl.BlockSpec((2 * rows, 128), lambda i, chunk, place: (chunk[i], 0))
    flat = [pieces[key] for parts in names for key in parts]
    return pl.pallas_call(
        functools.partial(update_kernel, names, rows),
        grid_spec=pltpu.PrefetchScalarGridSpec(
            num_scalar_prefetch=2,
            grid=(len(names),),
            in_specs=[block] + vmem(2 + len(flat)),
            out_specs=block,
            scratch_shapes=[pltpu.VMEM((rows, 256), F32)],
        ),
        out_shape=jax.ShapeDtypeStruct(x.shape, F32),
        compiler_params=pltpu.CompilerParams(vmem_limit_bytes=40 * 1024 * 1024),
    )(chunks, jnp.stack([row, col]).astype(jnp.int32), x, m, special, *flat)


def body(slab):
    row, col = lax.axis_index("row"), lax.axis_index("col")
    x = slab.reshape(slab.shape[0] * 128 * 2, 128)
    rows = x.shape[0] // (2 * PIECES)
    own = extract(x, jnp.asarray(ORDER)[col], rows)
    heads = lax.all_gather(x[:256].reshape(128, 256), "row", axis=0)
    head = heads[:2].reshape(256, 256)
    pieces = spread(own, col)
    whole = corner(head[:, :128], col)
    m, special = factor_all(whole, head, row, col)
    names = [((0, 0),)] + [(key,) for key in pieces if key != (0, 0) and len(key) == 2]
    names.append(((0, 2, 1), (0, 2, 2)))
    where = np.zeros((CHIPS, len(names)), np.int32)
    for chip in range(CHIPS):
        z, y = place(chip)
        where[chip] = [CLASS_OF[at(z + n[0][0], y + n[0][1])] for n in names]
    chunks = jnp.asarray(where)[col]
    out = update(x, m, special, pieces, chunks, row, col, names, rows)
    return out.reshape(slab.shape)


def solution(mesh):
    spec = P(None, "row", None, None, "col", None)
    return jax.shard_map(body, mesh=mesh, in_specs=(spec,), out_specs=spec, check_vma=False)
```

```python
import functools

import jax
import jax.numpy as jnp
import numpy as np
from jax import lax
from jax.experimental import pallas as pl
from jax.experimental.pallas import tpu as pltpu
from jax.sharding import PartitionSpec as P

F32 = jnp.float32
BF16 = jnp.bfloat16
NZ, NY = 8, 4
ROWS = 8
ROOTS = (0, 1)
SUBROOTS = ((0, 0), (0, 3), (2, 0), (6, 0))
QUARTERS = ((0, 0), (0, 2), (2, 1), (2, 3), (0, 1), (0, 3), (1, 3), (3, 0), (1, 1), (1, 2), (2, 0), (3, 3), (1, 0), (2, 2), (3, 1), (3, 2))
DELIVER = (
    ((0, 9, 2, 0), (1, 10, 3, 1), (2, 16, 1, 1), (3, 19, 0, 0), (8, 15, 3, 0), (9, 28, 3, 1), (24, 13, 2, 0), (25, 29, 3, 1)),
    ((0, 27, 2, 0), (1, 24, 3, 1), (2, 31, 3, 1), (3, 17, 1, 0), (8, 6, 1, 0), (9, 4, 0, 1), (24, 14, 3, 0), (25, 12, 2, 1)),
    ((0, 25, 3, 0), (1, 26, 2, 1), (2, 0, 0, 1), (3, 1, 0, 0), (8, 23, 0, 0), (9, 22, 0, 1), (24, 10, 1, 0), (25, 11, 1, 1)),
    ((0, 2, 1, 0), (1, 8, 2, 1), (2, 6, 2, 1), (3, 30, 3, 0), (8, 26, 2, 0), (9, 14, 3, 1), (24, 28, 3, 0), (25, 5, 0, 1)),
    ((0, 11, 3, 0), (1, 17, 1, 1), (2, 18, 0, 1), (3, 21, 2, 0), (8, 5, 0, 0), (9, 27, 2, 1), (24, 4, 0, 0), (25, 15, 3, 1)),
    ((0, 16, 1, 0), (1, 3, 1, 1), (2, 20, 2, 1), (3, 12, 3, 0), (8, 29, 3, 0), (9, 7, 1, 1), (24, 31, 2, 0), (25, 23, 0, 1)),
    ((0, 18, 0, 0), (1, 19, 0, 1), (2, 13, 3, 1), (3, 7, 2, 0), (8, 20, 1, 0), (9, 21, 1, 1), (24, 22, 0, 0), (25, 30, 2, 1)),
)


WORKERS = (20, 21)


def at(z, y):
    return (z % NZ) * NY + y % NY


def seen_from(root, z, y):
    return at(z, y) if root == 0 else at(z, ROOTS[1] - y)


def place(chip):
    return chip // NY, chip % NY


PIECES = 16
CHIPS = NZ * NY


def class_of(z, y):
    z, y = z & (NZ - 1), y & (NY - 1)
    return (z & 3) * 4 + ((y + ((z >> 2) << 1)) & 3)


def is_in(chips, chip):
    return ((jnp.uint32(sum(1 << c for c in chips)) >> chip.astype(jnp.uint32)) & 1) == 1


def lookup(slots, chip):
    low = is_in([c for c, slot in slots.items() if slot & 1], chip).astype(jnp.int32)
    high = is_in([c for c, slot in slots.items() if slot & 2], chip).astype(jnp.int32)
    return low + 2 * high


def extract_kernel(rows, where_ref, x_ref, *refs):
    outs, buffer, sem = refs[:-2], refs[-2], refs[-1]
    copies = []
    second = where_ref[1] == ROOTS[1]
    for k, (z, y) in enumerate(QUARTERS):
        piece = jnp.where(second, class_of(z, ROOTS[1] - y), class_of(z, y))
        start = pl.multiple_of(piece * (2 * rows), 2 * rows)
        copies.append(pltpu.make_async_copy(x_ref.at[pl.ds(start, 2 * rows)], buffer.at[k], sem.at[k]))
        copies[-1].start()
    for k, copy in enumerate(copies):
        copy.wait()
        outs[k // 4][k % 4] = buffer[k, pl.ds(0, rows, stride=2), :]


def extract(x, where, rows):
    return pl.pallas_call(
        functools.partial(extract_kernel, rows),
        out_shape=(jax.ShapeDtypeStruct((4, rows, 128), F32),) * 4,
        in_specs=[pl.BlockSpec(memory_space=pltpu.SMEM), pl.BlockSpec(memory_space=pltpu.HBM)],
        out_specs=tuple(vmem(4)),
        cost_estimate=cost(0, PIECES * rows * 3 * 2**9),
        scratch_shapes=[pltpu.VMEM((PIECES, 2 * rows, 128), F32), pltpu.SemaphoreType.DMA((PIECES,))],
        compiler_params=pltpu.CompilerParams(vmem_limit_bytes=60 * 1024 * 1024),
    )(where, x)


class Sender:
    def __init__(self, depth):
        self.depth = depth
        self.sent = []

    def __call__(self, value, pairs, axis="col"):
        if len(self.sent) >= self.depth:
            oldest = self.sent[-self.depth]
            value, oldest[0] = lax.optimization_barrier((value, oldest[0]))
        result = [lax.ppermute(value, axis, pairs)]
        self.sent.append(result)
        return result


def tie(*values):
    return lax.optimization_barrier(values)


def shift(fz, fy):
    return [(at(z + fz, y + fy), at(z, y)) for z in range(NZ) for y in range(NY)]


BOTH = ("col", "row")


def cores(pairs, shift=0):
    return [(a * ROWS + i, b * ROWS + 2 * shift + i) for a, b in pairs for i in (0, 1)]


def to_workers(send, block, row):
    swap = [(root * ROWS + i, root * ROWS + 1 - i) for root in ROOTS for i in (0, 1)]
    other = send(block, swap, BOTH)[0]
    pair = jnp.where(row == 0, jnp.concatenate([block, other]), jnp.concatenate([other, block]))
    return send(pair, cores(zip(ROOTS, WORKERS)), BOTH)


def scatter(send, own, got, row, chip):
    quarters = [
        send(own[k], [(root, seen_from(p, *SUBROOTS[k])) for p, root in enumerate(ROOTS)]) for k in (1, 2, 3)
    ]
    got = got[0]
    other = send(got, cores([WORKERS, WORKERS[::-1]]), BOTH)[0]
    quarter = jnp.where(chip < 2, own[0], sum(q[0] for q in quarters))
    arrived = []

    def deal(count):
        for _ in range(count):
            sends = DELIVER[len(arrived)]
            slot = lookup({source: slot for source, _, slot, _ in sends}, chip)
            value = lax.dynamic_index_in_dim(quarter, slot, 0, keepdims=False)
            arrived.append(send(value, [(source, target) for source, target, _, _ in sends]))

    deal(4)
    first, second = jnp.where(chip == WORKERS[0], got, other), jnp.where(chip == WORKERS[0], other, got)
    whole = jnp.concatenate([first, second[128:]])
    factor = lax.cond(is_in(WORKERS, chip) & (row < 2), factor_corner, jnp.zeros_like, whole)
    factor, quarter = tie(factor, quarter)
    deal(1)
    factor = factor + sum(send(factor, cores([(w, w) for w in WORKERS], k), BOTH)[0] for k in (1, 3, 2))
    deal(len(DELIVER) - len(arrived))
    places = {}
    for panel in (0, 1):
        for k, (pz, py) in enumerate(SUBROOTS):
            kinds = [class_of(*m) for m in QUARTERS[4 * k : 4 * k + 4]]
            places[seen_from(panel, pz, py)] = kinds.index(class_of(pz, py))
    held = lax.dynamic_index_in_dim(quarter, lookup(places, chip), 0, keepdims=False)
    mine = []
    for panel in (0, 1):
        value = held
        for k, sends in enumerate(DELIVER):
            got = is_in([target for _, target, _, p in sends if p == panel], chip)
            value = jnp.where(got, arrived[k][0], value)
        mine.append(value)
    return jnp.stack(mine), factor


def share_far(send, factor):
    z, y = place(WORKERS[0])
    line = send(factor, [(at(z, y), at(z, y - 1)), (at(z, y + 1), at(z, y + 2))])[0]
    line = factor + line
    far = send(line, [(at(z, j), at(z + 3, j)) for j in range(NY)])
    back = send(line, [(at(z, j), at(z - 3, j)) for j in range(NY)])
    return line + far[0] + back[0]


def share_near(send, base, chip):
    z = place(WORKERS[0])[0]
    above = send(base, [(at(z + k, j), at(z + k + 1, j)) for k in (0, 3, -3) for j in range(NY)])
    below = send(base, [(at(z + k, j), at(z + k - 1, j)) for k in (0, 3) for j in range(NY)])
    return base + above[0] + below[0]


def dot(a, b, dims):
    return lax.dot_general(
        a, b, ((dims[:1], dims[1:]), ((), ())), precision=lax.Precision.HIGHEST, preferred_element_type=F32
    )


def eliminate(block):
    n = block.shape[0]
    block = 0.5 * (block + block.T)
    row_id = lax.broadcasted_iota(jnp.int32, (8, n), 0)
    lane_id = lax.broadcasted_iota(jnp.int32, (8, n), 1)
    left = [block[8 * k : 8 * k + 8] for k in range(n // 8)]
    right = [jnp.where(lane_id == row_id + 8 * k, 1.0, 0.0).astype(F32) for k in range(n // 8)]
    spread_rows = lambda v, r: jnp.broadcast_to(v[r : r + 1, :], (8, n))
    spread_lanes = lambda v, j: jnp.broadcast_to(v[:, j : j + 1], (8, n))
    for j in range(0, n, 2):
        k0, r = j // 8, j % 8
        lanes0 = [spread_lanes(left[k], j) for k in range(k0, n // 8)]
        lanes1 = [spread_lanes(left[k], j + 1) for k in range(k0, n // 8)]
        a, b, c = spread_rows(lanes0[0], r), spread_rows(lanes0[0], r + 1), spread_rows(lanes1[0], r + 1)
        over = 1.0 / (a * c - b * b)
        done = []
        for part in (left, right):
            row0, row1 = spread_rows(part[k0], r), spread_rows(part[k0], r + 1)
            u0, u1 = (c * row0 - b * row1) * over, (a * row1 - b * row0) * over
            done.append((row0, row1))
            for k in range(k0, n // 8):
                new = part[k] - (lanes0[k - k0] * u0 + lanes1[k - k0] * u1)
                part[k] = jnp.where(row_id > r + 1, new, part[k]) if k == k0 else new
        first = 1.0 / jnp.sqrt(a)
        ratio = b / a
        second = 1.0 / jnp.sqrt(c - b * ratio)
        row0, row1 = done[1]
        right[k0] = jnp.where(
            row_id == r, row0 * first, jnp.where(row_id == r + 1, (row1 - ratio * row0) * second, right[k0])
        )
    return jnp.concatenate(right, axis=0)


def factor_kernel(a_ref, o_ref):
    inverse = eliminate(a_ref[:128])
    o_ref[:128] = inverse
    low = dot(a_ref[128:256], inverse, (1, 1))
    o_ref[128:256] = low
    o_ref[256:] = eliminate(a_ref[256:] - dot(low, low, (1, 1)))


def combine_kernel(place_ref, head_ref, f_ref, m_ref, s_ref):
    row, col = place_ref[0], place_ref[1]
    w0, low, w1 = f_ref[:128], f_ref[128:256], f_ref[256:]
    head0, head1 = head_ref[0], head_ref[1]
    g0 = dot(w0, head0, (1, 0))
    rest = head1 - dot(low, g0, (1, 0))
    g1 = dot(w1, rest, (1, 0))
    m1 = dot(w1, g1, (0, 0))
    m0 = dot(w0, g0 - dot(low, m1, (0, 0)), (0, 0))
    mixed = dot(w0, dot(low, w1, (0, 1)), (0, 0))
    zero = jnp.zeros((128, 128), F32)
    root0, root1 = col == ROOTS[0], col == ROOTS[1]
    m_ref[:128, 128:] = m0[:, 128:]
    m_ref[128:, 128:] = m1[:, 128:]
    m_ref[:128, :128] = jnp.where(root0, -w0.T, jnp.where(root1, mixed, m0[:, :128]))
    m_ref[128:, :128] = jnp.where(root0, zero, jnp.where(root1, -w1.T, m1[:, :128]))
    top = row == 0
    s_ref[:, 128:] = jnp.where(top, head0[:, 128:], rest[:, 128:])
    normal = jnp.where(top, head0[:, :128], rest[:, :128])
    lower = lax.broadcasted_iota(jnp.int32, (128, 128), 0) >= lax.broadcasted_iota(jnp.int32, (128, 128), 1)
    diagonal = jnp.where(top, dot(head0[:, :128], w0, (1, 1)), dot(rest[:, :128], w1, (1, 1)))
    diagonal = jnp.where(lower, diagonal, 0.0)
    on0 = jnp.where(top, diagonal, low)
    on1 = jnp.where(top, zero, diagonal)
    s_ref[:, :128] = jnp.where(root0, on0, jnp.where(root1, on1, normal))


def cost(flops, size):
    return pl.CostEstimate(flops=flops, bytes_accessed=size, transcendentals=0)


def vmem(count):
    return [pl.BlockSpec(memory_space=pltpu.VMEM)] * count


def factor_corner(whole):
    return pl.pallas_call(
        factor_kernel,
        out_shape=jax.ShapeDtypeStruct((384, 128), F32),
        in_specs=vmem(1),
        out_specs=vmem(1)[0],
        cost_estimate=cost(24 * 10**9, 6 * 2**16),
    )(whole)


def combine(heads, factor, where):
    return pl.pallas_call(
        combine_kernel,
        out_shape=(jax.ShapeDtypeStruct((256, 256), F32), jax.ShapeDtypeStruct((128, 256), F32)),
        grid=(1,),
        in_specs=[pl.BlockSpec(memory_space=pltpu.SMEM), pl.BlockSpec((2, 128, 256), lambda i: (0, 0, 0))] + vmem(1),
        out_specs=tuple(vmem(2)),
        cost_estimate=cost(4 * 10**9, 2**20),
    )(where, heads, factor)


def update_kernel(parts, keys, rows, aliased, place_ref, x_ref, m_ref, s_ref, *refs):
    count = len(parts)
    o_ref, xs, wide, chunk_ref, x_sem, p_sem, o_sem = refs[-7:]
    pieces = refs[: len(refs) - 7 - (1 if aliased else 0)]
    col_z, col_y = place_ref[1] >> 2, place_ref[1] & 3
    for k, (z, y) in enumerate(keys):
        chunk_ref[k] = class_of(col_z + z, col_y + y)

    def rows_of(ref, k):
        return ref.at[pl.ds(pl.multiple_of(chunk_ref[k] * (2 * rows), 2 * rows), 2 * rows)]

    def x_copy(k):
        return pltpu.make_async_copy(rows_of(x_ref, k), xs.at[k], x_sem.at[k])

    def o_copy(k):
        return pltpu.make_async_copy(xs.at[k], rows_of(o_ref, k), o_sem.at[k])

    for k, sources in enumerate(parts):
        x_copy(k).start()
        start = 0
        for which, offset, size in sources:
            for panel in (0, 1):
                pltpu.make_async_copy(
                    pieces[which].at[panel, pl.ds(offset, size)],
                    wide.at[k, pl.ds(start, size), pl.ds(128 * panel, 128)],
                    p_sem.at[k],
                ).start()
            start += size
    m = m_ref[...]
    m_high = m.astype(BF16)
    m_rest = (m - m_high.astype(F32)).astype(BF16)
    m_wide = jnp.concatenate([m_high, m_high, m_rest], axis=0)
    root = place_ref[1] < 2

    def step(k, carry):
        pltpu.make_async_copy(wide.at[k], wide.at[k], p_sem.at[k]).wait()
        value = wide[k]
        high = value.astype(BF16)
        rest = (value - high.astype(F32)).astype(BF16)
        product = jnp.dot(
            jnp.concatenate([high, rest, high], axis=1), m_wide, preferred_element_type=F32
        )
        x_copy(k).wait()
        left = xs[k, pl.ds(0, rows, stride=2), :]
        xs[k, pl.ds(0, rows, stride=2), :] = jnp.where(root, 0.0, left) - product[:, :128]
        xs[k, pl.ds(1, rows, stride=2), :] = xs[k, pl.ds(1, rows, stride=2), :] - product[:, 128:]

        @pl.when((chunk_ref[k] == 0) & (place_ref[0] < 2))
        def _():
            xs[k, pl.ds(0, 128, stride=2), :] = s_ref[:, :128]
            xs[k, pl.ds(1, 128, stride=2), :] = s_ref[:, 128:]

        o_copy(k).start()
        return carry

    lax.fori_loop(0, count, step, 0)

    def finish(k, carry):
        o_copy(k).wait()
        return carry

    lax.fori_loop(0, count, finish, 0)


def update(x, m, special, parts, keys, where, rows, out=None):
    arrays = []
    for sources in parts:
        for array, _, _ in sources:
            if not any(array is other for other in arrays):
                arrays.append(array)
    place_of = lambda array: [other is array for other in arrays].index(True)
    parts = [tuple((place_of(array), offset, size) for array, offset, size in sources) for sources in parts]
    count = len(parts)
    in_hbm = [pl.BlockSpec(memory_space=pltpu.HBM)]
    operands = [where, x, m, special, *arrays] + ([] if out is None else [out])
    return pl.pallas_call(
        functools.partial(update_kernel, parts, keys, rows, out is not None),
        out_shape=jax.ShapeDtypeStruct(x.shape, F32),
        in_specs=[pl.BlockSpec(memory_space=pltpu.SMEM)]
        + in_hbm
        + vmem(2)
        + [pl.BlockSpec(memory_space=pl.ANY)] * (len(operands) - 4),
        out_specs=in_hbm[0],
        scratch_shapes=[
            pltpu.VMEM((count, 2 * rows, 128), F32),
            pltpu.VMEM((count, rows, 256), F32),
            pltpu.SMEM((count,), jnp.int32),
            pltpu.SemaphoreType.DMA((count,)),
            pltpu.SemaphoreType.DMA((count,)),
            pltpu.SemaphoreType.DMA((count,)),
        ],
        cost_estimate=cost(count * rows * 2**18, count * rows * 3 * 2**10),
        input_output_aliases={} if out is None else {len(operands) - 1: 0},
        compiler_params=pltpu.CompilerParams(vmem_limit_bytes=60 * 1024 * 1024),
    )(*operands)


def body(slab):
    row, col = lax.axis_index("row"), lax.axis_index("col")
    x = slab.reshape(slab.shape[0] * 128 * 2, 128)
    rows = x.shape[0] // (2 * PIECES)
    half = rows // 2
    where = jnp.stack([row, col]).astype(jnp.int32)
    top, x = tie(x[:256].reshape(128, 256), x)
    send = Sender(5)
    got = to_workers(send, top[:, :128], row)
    own = extract(x, where, rows)
    heads = lax.all_gather(top, "row", axis=0)
    mine, factor = scatter(send, own, got, row, col)

    north, south = send(mine, shift(1, 0)), send(mine, shift(-1, 0))
    east, west = send(mine, shift(0, 1)), send(mine, shift(0, -1))
    factor = share_far(send, factor)
    north, south, east, west = north[0], south[0], east[0], west[0]
    north2, south2 = send(north, shift(1, 0)), send(south, shift(-1, 0))
    east2 = send(jnp.concatenate([north, south, east[:, :half]], axis=1), shift(0, 1))
    west2 = send(jnp.concatenate([north, south, west[:, half:]], axis=1), shift(0, -1))
    factor = share_near(send, factor, col)
    north2, south2 = north2[0], south2[0]
    north3, south3 = send(north2, shift(1, 0)), send(south2, shift(-1, 0))
    m, special = combine(heads, factor, where)
    east2 = east2[0]
    corner0, corner1 = send(east2[:, :rows], shift(1, 0)), send(east2[:, rows : 2 * rows], shift(-1, 0))

    def whole_piece(array):
        return ((array, 0, rows),)

    keys = [(0, 0), (1, 0), (-1, 0), (0, 1), (0, -1), (2, 0), (-2, 0)]
    parts = [whole_piece(v) for v in (mine, north, south, east, west, north2, south2)]
    out = update(x, m, special, parts, keys, where, rows)
    west2, north3, south3 = west2[0], north3[0], south3[0]
    keys = [(1, 1), (-1, 1), (1, -1), (-1, -1), (0, 2), (3, 0), (-3, 0)]
    parts = [((v, k * rows, rows),) for v in (east2, west2) for k in (0, 1)]
    parts += [((east2, 2 * rows, half), (west2, 2 * rows, half)), whole_piece(north3), whole_piece(south3)]
    out = update(x, m, special, parts, keys, where, rows, out)
    parts = [whole_piece(corner0[0]), whole_piece(corner1[0])]
    out = update(x, m, special, parts, [(2, 1), (-2, 1)], where, rows, out)
    return out.reshape(slab.shape)


def solution(mesh):
    spec = P(None, "row", None, None, "col", None)
    return jax.shard_map(body, mesh=mesh, in_specs=(spec,), out_specs=spec, check_vma=False)
```

```python
import functools

import jax
import jax.numpy as jnp
import numpy as np
from jax import lax
from jax.experimental import pallas as pl
from jax.experimental.pallas import tpu as pltpu
from jax.sharding import PartitionSpec as P

F32 = jnp.float32
BF16 = jnp.bfloat16
NZ, NY = 8, 4
ROWS = 8
ROOTS = (0, 1)
SUBROOTS = ((0, 0), (0, 3), (2, 0), (6, 0))
QUARTERS = ((0, 0), (0, 2), (2, 1), (2, 3), (0, 1), (0, 3), (1, 3), (3, 0), (1, 1), (1, 2), (2, 0), (3, 3), (1, 0), (2, 2), (3, 1), (3, 2))
DELIVER = (
    ((0, 9, 2, 0), (1, 10, 3, 1), (2, 16, 1, 1), (3, 19, 0, 0), (8, 15, 3, 0), (9, 28, 3, 1), (24, 13, 2, 0), (25, 29, 3, 1)),
    ((0, 27, 2, 0), (1, 24, 3, 1), (2, 31, 3, 1), (3, 17, 1, 0), (8, 6, 1, 0), (9, 4, 0, 1), (24, 14, 3, 0), (25, 12, 2, 1)),
    ((0, 25, 3, 0), (1, 26, 2, 1), (2, 0, 0, 1), (3, 1, 0, 0), (8, 23, 0, 0), (9, 22, 0, 1), (24, 10, 1, 0), (25, 11, 1, 1)),
    ((0, 2, 1, 0), (1, 8, 2, 1), (2, 6, 2, 1), (3, 30, 3, 0), (8, 26, 2, 0), (9, 14, 3, 1), (24, 28, 3, 0), (25, 5, 0, 1)),
    ((0, 11, 3, 0), (1, 17, 1, 1), (2, 18, 0, 1), (3, 21, 2, 0), (8, 5, 0, 0), (9, 27, 2, 1), (24, 4, 0, 0), (25, 15, 3, 1)),
    ((0, 16, 1, 0), (1, 3, 1, 1), (2, 20, 2, 1), (3, 12, 3, 0), (8, 29, 3, 0), (9, 7, 1, 1), (24, 31, 2, 0), (25, 23, 0, 1)),
    ((0, 18, 0, 0), (1, 19, 0, 1), (2, 13, 3, 1), (3, 7, 2, 0), (8, 20, 1, 0), (9, 21, 1, 1), (24, 22, 0, 0), (25, 30, 2, 1)),
)


WORKERS = (20, 21)


def at(z, y):
    return (z % NZ) * NY + y % NY


def seen_from(root, z, y):
    return at(z, y) if root == 0 else at(z, ROOTS[1] - y)


def place(chip):
    return chip // NY, chip % NY


PIECES = 16
CHIPS = NZ * NY


def class_of(z, y):
    z, y = z & (NZ - 1), y & (NY - 1)
    return (z & 3) * 4 + ((y + ((z >> 2) << 1)) & 3)


def is_in(chips, chip):
    return ((jnp.uint32(sum(1 << c for c in chips)) >> chip.astype(jnp.uint32)) & 1) == 1


def lookup(slots, chip):
    low = is_in([c for c, slot in slots.items() if slot & 1], chip).astype(jnp.int32)
    high = is_in([c for c, slot in slots.items() if slot & 2], chip).astype(jnp.int32)
    return low + 2 * high


def extract_kernel(rows, where_ref, x_ref, *refs):
    outs, buffer, sem = refs[:-2], refs[-2], refs[-1]
    copies = []
    second = where_ref[1] == ROOTS[1]
    for k, (z, y) in enumerate(QUARTERS):
        piece = jnp.where(second, class_of(z, ROOTS[1] - y), class_of(z, y))
        start = pl.multiple_of(piece * (2 * rows), 2 * rows)
        copies.append(pltpu.make_async_copy(x_ref.at[pl.ds(start, 2 * rows)], buffer.at[k], sem.at[k]))
        copies[-1].start()
    for k, copy in enumerate(copies):
        copy.wait()
        outs[k // 4][k % 4] = buffer[k, pl.ds(0, rows, stride=2), :]


def extract(x, where, rows):
    return pl.pallas_call(
        functools.partial(extract_kernel, rows),
        out_shape=(jax.ShapeDtypeStruct((4, rows, 128), F32),) * 4,
        in_specs=[pl.BlockSpec(memory_space=pltpu.SMEM), pl.BlockSpec(memory_space=pltpu.HBM)],
        out_specs=tuple(vmem(4)),
        cost_estimate=cost(0, PIECES * rows * 3 * 2**9),
        scratch_shapes=[pltpu.VMEM((PIECES, 2 * rows, 128), F32), pltpu.SemaphoreType.DMA((PIECES,))],
        compiler_params=pltpu.CompilerParams(vmem_limit_bytes=60 * 1024 * 1024),
    )(where, x)


class Sender:
    def __init__(self, depth):
        self.depth = depth
        self.sent = []

    def __call__(self, value, pairs, axis="col"):
        if len(self.sent) >= self.depth:
            oldest = self.sent[-self.depth]
            value, oldest[0] = lax.optimization_barrier((value, oldest[0]))
        result = [lax.ppermute(value, axis, pairs)]
        self.sent.append(result)
        return result


def tie(*values):
    return lax.optimization_barrier(values)


def shift(fz, fy):
    return [(at(z + fz, y + fy), at(z, y)) for z in range(NZ) for y in range(NY)]


BOTH = ("col", "row")


def cores(pairs, shift=0):
    return [(a * ROWS + i, b * ROWS + 2 * shift + i) for a, b in pairs for i in (0, 1)]


def to_workers(send, block, row):
    swap = [(root * ROWS + i, root * ROWS + 1 - i) for root in ROOTS for i in (0, 1)]
    other = send(block, swap, BOTH)[0]
    pair = jnp.where(row == 0, jnp.concatenate([block, other]), jnp.concatenate([other, block]))
    return send(pair, cores(zip(ROOTS, WORKERS)), BOTH)


def scatter(send, own, got, row, chip):
    quarters = [
        send(own[k], [(root, seen_from(p, *SUBROOTS[k])) for p, root in enumerate(ROOTS)]) for k in (1, 2, 3)
    ]
    got = got[0]
    other = send(got, cores([WORKERS, WORKERS[::-1]]), BOTH)[0]
    quarter = jnp.where(chip < 2, own[0], sum(q[0] for q in quarters))
    arrived = []

    def deal(count):
        for _ in range(count):
            sends = DELIVER[len(arrived)]
            slot = lookup({source: slot for source, _, slot, _ in sends}, chip)
            value = lax.dynamic_index_in_dim(quarter, slot, 0, keepdims=False)
            arrived.append(send(value, [(source, target) for source, target, _, _ in sends]))

    deal(4)
    first, second = jnp.where(chip == WORKERS[0], got, other), jnp.where(chip == WORKERS[0], other, got)
    whole = jnp.concatenate([first, second[128:]])
    factor = lax.cond(is_in(WORKERS, chip) & (row < 2), factor_corner, jnp.zeros_like, whole)
    factor, quarter = tie(factor, quarter)
    deal(1)
    factor = factor + sum(send(factor, cores([(w, w) for w in WORKERS], k), BOTH)[0] for k in (1, 3, 2))
    deal(len(DELIVER) - len(arrived))
    places = {}
    for panel in (0, 1):
        for k, (pz, py) in enumerate(SUBROOTS):
            kinds = [class_of(*m) for m in QUARTERS[4 * k : 4 * k + 4]]
            places[seen_from(panel, pz, py)] = kinds.index(class_of(pz, py))
    held = lax.dynamic_index_in_dim(quarter, lookup(places, chip), 0, keepdims=False)
    mine = []
    for panel in (0, 1):
        value = held
        for k, sends in enumerate(DELIVER):
            got = is_in([target for _, target, _, p in sends if p == panel], chip)
            value = jnp.where(got, arrived[k][0], value)
        mine.append(value)
    return jnp.stack(mine), factor


def share_far(send, factor):
    z, y = place(WORKERS[0])
    line = send(factor, [(at(z, y), at(z, y - 1)), (at(z, y + 1), at(z, y + 2))])[0]
    line = factor + line
    far = send(line, [(at(z, j), at(z + 3, j)) for j in range(NY)])
    back = send(line, [(at(z, j), at(z - 3, j)) for j in range(NY)])
    return line + far[0] + back[0]


def share_near(send, base, chip):
    z = place(WORKERS[0])[0]
    above = send(base, [(at(z + k, j), at(z + k + 1, j)) for k in (0, 3, -3) for j in range(NY)])
    below = send(base, [(at(z + k, j), at(z + k - 1, j)) for k in (0, 3) for j in range(NY)])
    return base + above[0] + below[0]


def dot(a, b, dims):
    return lax.dot_general(
        a, b, ((dims[:1], dims[1:]), ((), ())), precision=lax.Precision.HIGHEST, preferred_element_type=F32
    )


def eliminate(block):
    n = block.shape[0]
    block = 0.5 * (block + block.T)
    row_id = lax.broadcasted_iota(jnp.int32, (8, n), 0)
    lane_id = lax.broadcasted_iota(jnp.int32, (8, n), 1)
    left = [block[8 * k : 8 * k + 8] for k in range(n // 8)]
    right = [jnp.where(lane_id == row_id + 8 * k, 1.0, 0.0).astype(F32) for k in range(n // 8)]
    spread_rows = lambda v, r: jnp.broadcast_to(v[r : r + 1, :], (8, n))
    spread_lanes = lambda v, j: jnp.broadcast_to(v[:, j : j + 1], (8, n))
    for j in range(0, n, 2):
        k0, r = j // 8, j % 8
        lanes0 = [spread_lanes(left[k], j) for k in range(k0, n // 8)]
        lanes1 = [spread_lanes(left[k], j + 1) for k in range(k0, n // 8)]
        a, b, c = spread_rows(lanes0[0], r), spread_rows(lanes0[0], r + 1), spread_rows(lanes1[0], r + 1)
        over = 1.0 / (a * c - b * b)
        done = []
        for part in (left, right):
            row0, row1 = spread_rows(part[k0], r), spread_rows(part[k0], r + 1)
            u0, u1 = (c * row0 - b * row1) * over, (a * row1 - b * row0) * over
            done.append((row0, row1))
            for k in range(k0, n // 8):
                new = part[k] - (lanes0[k - k0] * u0 + lanes1[k - k0] * u1)
                part[k] = jnp.where(row_id > r + 1, new, part[k]) if k == k0 else new
        first = 1.0 / jnp.sqrt(a)
        ratio = b / a
        second = 1.0 / jnp.sqrt(c - b * ratio)
        row0, row1 = done[1]
        right[k0] = jnp.where(
            row_id == r, row0 * first, jnp.where(row_id == r + 1, (row1 - ratio * row0) * second, right[k0])
        )
    return jnp.concatenate(right, axis=0)


def factor_kernel(a_ref, o_ref):
    inverse = eliminate(a_ref[:128])
    o_ref[:128] = inverse
    low = dot(a_ref[128:256], inverse, (1, 1))
    o_ref[128:256] = low
    o_ref[256:] = eliminate(a_ref[256:] - dot(low, low, (1, 1)))


def combine_kernel(place_ref, head_ref, f_ref, m_ref, s_ref):
    row, col = place_ref[0], place_ref[1]
    w0, low, w1 = f_ref[:128], f_ref[128:256], f_ref[256:]
    head0, head1 = head_ref[0], head_ref[1]
    g0 = dot(w0, head0, (1, 0))
    rest = head1 - dot(low, g0, (1, 0))
    g1 = dot(w1, rest, (1, 0))
    m1 = dot(w1, g1, (0, 0))
    m0 = dot(w0, g0 - dot(low, m1, (0, 0)), (0, 0))
    mixed = dot(w0, dot(low, w1, (0, 1)), (0, 0))
    zero = jnp.zeros((128, 128), F32)
    root0, root1 = col == ROOTS[0], col == ROOTS[1]
    m_ref[:128, 128:] = m0[:, 128:]
    m_ref[128:, 128:] = m1[:, 128:]
    m_ref[:128, :128] = jnp.where(root0, -w0.T, jnp.where(root1, mixed, m0[:, :128]))
    m_ref[128:, :128] = jnp.where(root0, zero, jnp.where(root1, -w1.T, m1[:, :128]))
    top = row == 0
    s_ref[:, 128:] = jnp.where(top, head0[:, 128:], rest[:, 128:])
    normal = jnp.where(top, head0[:, :128], rest[:, :128])
    lower = lax.broadcasted_iota(jnp.int32, (128, 128), 0) >= lax.broadcasted_iota(jnp.int32, (128, 128), 1)
    diagonal = jnp.where(top, dot(head0[:, :128], w0, (1, 1)), dot(rest[:, :128], w1, (1, 1)))
    diagonal = jnp.where(lower, diagonal, 0.0)
    on0 = jnp.where(top, diagonal, low)
    on1 = jnp.where(top, zero, diagonal)
    s_ref[:, :128] = jnp.where(root0, on0, jnp.where(root1, on1, normal))


def cost(flops, size):
    return pl.CostEstimate(flops=flops, bytes_accessed=size, transcendentals=0)


def vmem(count):
    return [pl.BlockSpec(memory_space=pltpu.VMEM)] * count


def factor_corner(whole):
    return pl.pallas_call(
        factor_kernel,
        out_shape=jax.ShapeDtypeStruct((384, 128), F32),
        in_specs=vmem(1),
        out_specs=vmem(1)[0],
        cost_estimate=cost(24 * 10**9, 6 * 2**16),
    )(whole)


def combine(heads, factor, where):
    return pl.pallas_call(
        combine_kernel,
        out_shape=(jax.ShapeDtypeStruct((256, 256), F32), jax.ShapeDtypeStruct((128, 256), F32)),
        grid=(1,),
        in_specs=[pl.BlockSpec(memory_space=pltpu.SMEM), pl.BlockSpec((2, 128, 256), lambda i: (0, 0, 0))] + vmem(1),
        out_specs=tuple(vmem(2)),
        cost_estimate=cost(4 * 10**9, 2**20),
    )(where, heads, factor)


def update_kernel(parts, keys, rows, aliased, place_ref, x_ref, m_ref, s_ref, *refs):
    count = len(parts)
    o_ref, xs, wide, chunk_ref, x_sem, p_sem, o_sem = refs[-7:]
    pieces = refs[: len(refs) - 7 - (1 if aliased else 0)]
    col_z, col_y = place_ref[1] >> 2, place_ref[1] & 3
    for k, (z, y) in enumerate(keys):
        chunk_ref[k] = class_of(col_z + z, col_y + y)

    def rows_of(ref, k):
        return ref.at[pl.ds(pl.multiple_of(chunk_ref[k] * (2 * rows), 2 * rows), 2 * rows)]

    def x_copy(k):
        return pltpu.make_async_copy(rows_of(x_ref, k), xs.at[k], x_sem.at[k])

    def o_copy(k):
        return pltpu.make_async_copy(xs.at[k], rows_of(o_ref, k), o_sem.at[k])

    for k, sources in enumerate(parts):
        x_copy(k).start()
        start = 0
        for which, offset, size in sources:
            for panel in (0, 1):
                pltpu.make_async_copy(
                    pieces[which].at[panel, pl.ds(offset, size)],
                    wide.at[k, pl.ds(start, size), pl.ds(128 * panel, 128)],
                    p_sem.at[k],
                ).start()
            start += size
    m = m_ref[...]
    m_high = m.astype(BF16)
    m_rest = (m - m_high.astype(F32)).astype(BF16)
    m_wide = jnp.concatenate([m_high, m_high, m_rest], axis=0)
    root = place_ref[1] < 2

    def step(k, carry):
        pltpu.make_async_copy(wide.at[k], wide.at[k], p_sem.at[k]).wait()
        value = wide[k]
        high = value.astype(BF16)
        rest = (value - high.astype(F32)).astype(BF16)
        product = jnp.dot(
            jnp.concatenate([high, rest, high], axis=1), m_wide, preferred_element_type=F32
        )
        x_copy(k).wait()
        left = xs[k, pl.ds(0, rows, stride=2), :]
        xs[k, pl.ds(0, rows, stride=2), :] = jnp.where(root, 0.0, left) - product[:, :128]
        xs[k, pl.ds(1, rows, stride=2), :] = xs[k, pl.ds(1, rows, stride=2), :] - product[:, 128:]

        @pl.when((chunk_ref[k] == 0) & (place_ref[0] < 2))
        def _():
            xs[k, pl.ds(0, 128, stride=2), :] = s_ref[:, :128]
            xs[k, pl.ds(1, 128, stride=2), :] = s_ref[:, 128:]

        o_copy(k).start()
        return carry

    lax.fori_loop(0, count, step, 0)

    def finish(k, carry):
        o_copy(k).wait()
        return carry

    lax.fori_loop(0, count, finish, 0)


def update(x, m, special, parts, keys, where, rows, out=None):
    arrays = []
    for sources in parts:
        for array, _, _ in sources:
            if not any(array is other for other in arrays):
                arrays.append(array)
    place_of = lambda array: [other is array for other in arrays].index(True)
    parts = [tuple((place_of(array), offset, size) for array, offset, size in sources) for sources in parts]
    count = len(parts)
    in_hbm = [pl.BlockSpec(memory_space=pltpu.HBM)]
    operands = [where, x, m, special, *arrays] + ([] if out is None else [out])
    return pl.pallas_call(
        functools.partial(update_kernel, parts, keys, rows, out is not None),
        out_shape=jax.ShapeDtypeStruct(x.shape, F32),
        in_specs=[pl.BlockSpec(memory_space=pltpu.SMEM)]
        + in_hbm
        + vmem(2)
        + [pl.BlockSpec(memory_space=pl.ANY)] * (len(operands) - 4),
        out_specs=in_hbm[0],
        scratch_shapes=[
            pltpu.VMEM((count, 2 * rows, 128), F32),
            pltpu.VMEM((count, rows, 256), F32),
            pltpu.SMEM((count,), jnp.int32),
            pltpu.SemaphoreType.DMA((count,)),
            pltpu.SemaphoreType.DMA((count,)),
            pltpu.SemaphoreType.DMA((count,)),
        ],
        cost_estimate=cost(count * rows * 2**18, count * rows * 3 * 2**10),
        input_output_aliases={} if out is None else {len(operands) - 1: 0},
        compiler_params=pltpu.CompilerParams(vmem_limit_bytes=60 * 1024 * 1024),
    )(*operands)


def body(slab):
    row, col = lax.axis_index("row"), lax.axis_index("col")
    x = slab.reshape(slab.shape[0] * 128 * 2, 128)
    rows = x.shape[0] // (2 * PIECES)
    half = rows // 2
    where = jnp.stack([row, col]).astype(jnp.int32)
    top, x = tie(x[:256].reshape(128, 256), x)
    send = Sender(5)
    got = to_workers(send, top[:, :128], row)
    own = extract(x, where, rows)
    heads = lax.all_gather(top, "row", axis=0)
    mine, factor = scatter(send, own, got, row, col)

    north, south = send(mine, shift(1, 0)), send(mine, shift(-1, 0))
    east, west = send(mine, shift(0, 1)), send(mine, shift(0, -1))
    north, south, east, west = north[0], south[0], east[0], west[0]
    north2, south2 = send(north, shift(1, 0)), send(south, shift(-1, 0))
    factor = share_far(send, factor)
    east2 = send(jnp.concatenate([north, south, east[:, :half]], axis=1), shift(0, 1))
    west2 = send(jnp.concatenate([north, south, west[:, half:]], axis=1), shift(0, -1))
    factor, north2, south2 = tie(factor, north2[0], south2[0])
    factor = share_near(send, factor, col)
    north3, south3 = send(north2, shift(1, 0)), send(south2, shift(-1, 0))
    m, special = combine(heads, factor, where)
    east2 = east2[0]
    corner0, corner1 = send(east2[:, :rows], shift(1, 0)), send(east2[:, rows : 2 * rows], shift(-1, 0))

    def whole_piece(array):
        return ((array, 0, rows),)

    west2, north3, south3 = west2[0], north3[0], south3[0]
    keys = [(0, 0), (1, 0), (-1, 0), (0, 1), (0, -1), (2, 0), (-2, 0), (3, 0), (-3, 0)]
    keys += [(1, 1), (-1, 1), (1, -1), (-1, -1), (0, 2)]
    parts = [whole_piece(v) for v in (mine, north, south, east, west, north2, south2, north3, south3)]
    parts += [((v, k * rows, rows),) for v in (east2, west2) for k in (0, 1)]
    parts += [((east2, 2 * rows, half), (west2, 2 * rows, half))]
    out = update(x, m, special, parts, keys, where, rows)
    parts = [whole_piece(corner0[0]), whole_piece(corner1[0])]
    out = update(x, m, special, parts, [(2, 1), (-2, 1)], where, rows, out)
    return out.reshape(slab.shape)


def solution(mesh):
    spec = P(None, "row", None, None, "col", None)
    return jax.shard_map(body, mesh=mesh, in_specs=(spec,), out_specs=spec, check_vma=False)
```

```python
import functools

import jax
import jax.numpy as jnp
import numpy as np
from jax import lax
from jax.experimental import pallas as pl
from jax.experimental.pallas import tpu as pltpu
from jax.sharding import PartitionSpec as P

F32 = jnp.float32
BF16 = jnp.bfloat16
NZ, NY = 8, 4
ROWS = 8
ROOTS = (0, 1)
SUBROOTS = ((0, 0), (0, 3), (2, 0), (6, 0))
QUARTERS = ((0, 0), (0, 2), (2, 1), (2, 3), (0, 1), (0, 3), (1, 3), (3, 0), (1, 1), (1, 2), (2, 0), (3, 3), (1, 0), (2, 2), (3, 1), (3, 2))
DELIVER = (
    ((0, 9, 2, 0), (1, 10, 3, 1), (2, 16, 1, 1), (3, 19, 0, 0), (8, 15, 3, 0), (9, 28, 3, 1), (24, 13, 2, 0), (25, 29, 3, 1)),
    ((0, 27, 2, 0), (1, 24, 3, 1), (2, 31, 3, 1), (3, 17, 1, 0), (8, 6, 1, 0), (9, 4, 0, 1), (24, 14, 3, 0), (25, 12, 2, 1)),
    ((0, 25, 3, 0), (1, 26, 2, 1), (2, 0, 0, 1), (3, 1, 0, 0), (8, 23, 0, 0), (9, 22, 0, 1), (24, 10, 1, 0), (25, 11, 1, 1)),
    ((0, 2, 1, 0), (1, 8, 2, 1), (2, 6, 2, 1), (3, 30, 3, 0), (8, 26, 2, 0), (9, 14, 3, 1), (24, 28, 3, 0), (25, 5, 0, 1)),
    ((0, 11, 3, 0), (1, 17, 1, 1), (2, 18, 0, 1), (3, 21, 2, 0), (8, 5, 0, 0), (9, 27, 2, 1), (24, 4, 0, 0), (25, 15, 3, 1)),
    ((0, 16, 1, 0), (1, 3, 1, 1), (2, 20, 2, 1), (3, 12, 3, 0), (8, 29, 3, 0), (9, 7, 1, 1), (24, 31, 2, 0), (25, 23, 0, 1)),
    ((0, 18, 0, 0), (1, 19, 0, 1), (2, 13, 3, 1), (3, 7, 2, 0), (8, 20, 1, 0), (9, 21, 1, 1), (24, 22, 0, 0), (25, 30, 2, 1)),
)


WORKERS = (20, 21)


def at(z, y):
    return (z % NZ) * NY + y % NY


def seen_from(root, z, y):
    return at(z, y) if root == 0 else at(z, ROOTS[1] - y)


def place(chip):
    return chip // NY, chip % NY


PIECES = 16
CHIPS = NZ * NY


def class_of(z, y):
    z, y = z & (NZ - 1), y & (NY - 1)
    return (z & 3) * 4 + ((y + ((z >> 2) << 1)) & 3)


def is_in(chips, chip):
    return ((jnp.uint32(sum(1 << c for c in chips)) >> chip.astype(jnp.uint32)) & 1) == 1


def lookup(slots, chip):
    low = is_in([c for c, slot in slots.items() if slot & 1], chip).astype(jnp.int32)
    high = is_in([c for c, slot in slots.items() if slot & 2], chip).astype(jnp.int32)
    return low + 2 * high


def extract_kernel(rows, where_ref, x_ref, *refs):
    outs, buffer, sem = refs[:-2], refs[-2], refs[-1]
    copies = []
    second = where_ref[1] == ROOTS[1]
    for k, (z, y) in enumerate(QUARTERS):
        piece = jnp.where(second, class_of(z, ROOTS[1] - y), class_of(z, y))
        start = pl.multiple_of(piece * (2 * rows), 2 * rows)
        copies.append(pltpu.make_async_copy(x_ref.at[pl.ds(start, 2 * rows)], buffer.at[k], sem.at[k]))
        copies[-1].start()
    for k, copy in enumerate(copies):
        copy.wait()
        outs[k // 4][k % 4] = buffer[k, pl.ds(0, rows, stride=2), :]


def extract(x, where, rows):
    return pl.pallas_call(
        functools.partial(extract_kernel, rows),
        out_shape=(jax.ShapeDtypeStruct((4, rows, 128), F32),) * 4,
        in_specs=[pl.BlockSpec(memory_space=pltpu.SMEM), pl.BlockSpec(memory_space=pltpu.HBM)],
        out_specs=tuple(vmem(4)),
        cost_estimate=cost(0, PIECES * rows * 3 * 2**9),
        scratch_shapes=[pltpu.VMEM((PIECES, 2 * rows, 128), F32), pltpu.SemaphoreType.DMA((PIECES,))],
        compiler_params=pltpu.CompilerParams(vmem_limit_bytes=60 * 1024 * 1024),
    )(where, x)


class Sender:
    def __init__(self, depth):
        self.depth = depth
        self.sent = []

    def __call__(self, value, pairs, axis="col"):
        if len(self.sent) >= self.depth:
            oldest = self.sent[-self.depth]
            value, oldest[0] = lax.optimization_barrier((value, oldest[0]))
        result = [lax.ppermute(value, axis, pairs)]
        self.sent.append(result)
        return result


def tie(*values):
    return lax.optimization_barrier(values)


def shift(fz, fy):
    return [(at(z + fz, y + fy), at(z, y)) for z in range(NZ) for y in range(NY)]


BOTH = ("col", "row")


def cores(pairs, shift=0):
    return [(a * ROWS + i, b * ROWS + 2 * shift + i) for a, b in pairs for i in (0, 1)]


def to_workers(send, block, row):
    swap = [(root * ROWS + i, root * ROWS + 1 - i) for root in ROOTS for i in (0, 1)]
    other = send(block, swap, BOTH)[0]
    pair = jnp.where(row == 0, jnp.concatenate([block, other]), jnp.concatenate([other, block]))
    return send(pair, cores(zip(ROOTS, WORKERS)), BOTH)


def scatter(send, own, got, row, chip):
    quarters = [
        send(own[k], [(root, seen_from(p, *SUBROOTS[k])) for p, root in enumerate(ROOTS)]) for k in (1, 2, 3)
    ]
    got = got[0]
    other = send(got, cores([WORKERS, WORKERS[::-1]]), BOTH)[0]
    quarter = jnp.where(chip < 2, own[0], sum(q[0] for q in quarters))
    arrived = []

    def deal(count):
        for _ in range(count):
            sends = DELIVER[len(arrived)]
            slot = lookup({source: slot for source, _, slot, _ in sends}, chip)
            value = lax.dynamic_index_in_dim(quarter, slot, 0, keepdims=False)
            arrived.append(send(value, [(source, target) for source, target, _, _ in sends]))

    deal(4)
    first, second = jnp.where(chip == WORKERS[0], got, other), jnp.where(chip == WORKERS[0], other, got)
    whole = jnp.concatenate([first, second[128:]])
    factor = lax.cond(is_in(WORKERS, chip) & (row < 2), factor_corner, jnp.zeros_like, whole)
    factor, quarter = tie(factor, quarter)
    deal(1)
    factor = factor + sum(send(factor, cores([(w, w) for w in WORKERS], k), BOTH)[0] for k in (1, 3, 2))
    deal(len(DELIVER) - len(arrived))
    places = {}
    for panel in (0, 1):
        for k, (pz, py) in enumerate(SUBROOTS):
            kinds = [class_of(*m) for m in QUARTERS[4 * k : 4 * k + 4]]
            places[seen_from(panel, pz, py)] = kinds.index(class_of(pz, py))
    held = lax.dynamic_index_in_dim(quarter, lookup(places, chip), 0, keepdims=False)
    mine = []
    for panel in (0, 1):
        value = held
        for k, sends in enumerate(DELIVER):
            got = is_in([target for _, target, _, p in sends if p == panel], chip)
            value = jnp.where(got, arrived[k][0], value)
        mine.append(value)
    return jnp.stack(mine), factor


def share_far(send, factor):
    z, y = place(WORKERS[0])
    line = send(factor, [(at(z, y), at(z, y - 1)), (at(z, y + 1), at(z, y + 2))])[0]
    line = factor + line
    far = send(line, [(at(z, j), at(z + 3, j)) for j in range(NY)])
    back = send(line, [(at(z, j), at(z - 3, j)) for j in range(NY)])
    return line + far[0] + back[0]


def share_near(send, base, chip):
    z = place(WORKERS[0])[0]
    above = send(base, [(at(z + k, j), at(z + k + 1, j)) for k in (0, 3, -3) for j in range(NY)])
    below = send(base, [(at(z + k, j), at(z + k - 1, j)) for k in (0, 3) for j in range(NY)])
    return base + above[0] + below[0]


def dot(a, b, dims):
    return lax.dot_general(
        a, b, ((dims[:1], dims[1:]), ((), ())), precision=lax.Precision.HIGHEST, preferred_element_type=F32
    )


def eliminate(block):
    n = block.shape[0]
    block = 0.5 * (block + block.T)
    row_id = lax.broadcasted_iota(jnp.int32, (8, n), 0)
    lane_id = lax.broadcasted_iota(jnp.int32, (8, n), 1)
    left = [block[8 * k : 8 * k + 8] for k in range(n // 8)]
    right = [jnp.where(lane_id == row_id + 8 * k, 1.0, 0.0).astype(F32) for k in range(n // 8)]
    spread_rows = lambda v, r: jnp.broadcast_to(v[r : r + 1, :], (8, n))
    spread_lanes = lambda v, j: jnp.broadcast_to(v[:, j : j + 1], (8, n))
    for j in range(0, n, 2):
        k0, r = j // 8, j % 8
        lanes0 = [spread_lanes(left[k], j) for k in range(k0, n // 8)]
        lanes1 = [spread_lanes(left[k], j + 1) for k in range(k0, n // 8)]
        a, b, c = spread_rows(lanes0[0], r), spread_rows(lanes0[0], r + 1), spread_rows(lanes1[0], r + 1)
        over = 1.0 / (a * c - b * b)
        done = []
        for part in (left, right):
            row0, row1 = spread_rows(part[k0], r), spread_rows(part[k0], r + 1)
            u0, u1 = (c * row0 - b * row1) * over, (a * row1 - b * row0) * over
            done.append((row0, row1))
            for k in range(k0, n // 8):
                new = part[k] - (lanes0[k - k0] * u0 + lanes1[k - k0] * u1)
                part[k] = jnp.where(row_id > r + 1, new, part[k]) if k == k0 else new
        first = 1.0 / jnp.sqrt(a)
        ratio = b / a
        second = 1.0 / jnp.sqrt(c - b * ratio)
        row0, row1 = done[1]
        right[k0] = jnp.where(
            row_id == r, row0 * first, jnp.where(row_id == r + 1, (row1 - ratio * row0) * second, right[k0])
        )
    return jnp.concatenate(right, axis=0)


def factor_kernel(a_ref, o_ref):
    inverse = eliminate(a_ref[:128])
    o_ref[:128] = inverse
    low = dot(a_ref[128:256], inverse, (1, 1))
    o_ref[128:256] = low
    o_ref[256:] = eliminate(a_ref[256:] - dot(low, low, (1, 1)))


def combine_kernel(place_ref, head_ref, f_ref, m_ref, s_ref):
    row, col = place_ref[0], place_ref[1]
    w0, low, w1 = f_ref[:128], f_ref[128:256], f_ref[256:]
    head0, head1 = head_ref[0], head_ref[1]
    g0 = dot(w0, head0, (1, 0))
    rest = head1 - dot(low, g0, (1, 0))
    g1 = dot(w1, rest, (1, 0))
    m1 = dot(w1, g1, (0, 0))
    m0 = dot(w0, g0 - dot(low, m1, (0, 0)), (0, 0))
    mixed = dot(w0, dot(low, w1, (0, 1)), (0, 0))
    zero = jnp.zeros((128, 128), F32)
    root0, root1 = col == ROOTS[0], col == ROOTS[1]
    m_ref[:128, 128:] = m0[:, 128:]
    m_ref[128:, 128:] = m1[:, 128:]
    m_ref[:128, :128] = jnp.where(root0, -w0.T, jnp.where(root1, mixed, m0[:, :128]))
    m_ref[128:, :128] = jnp.where(root0, zero, jnp.where(root1, -w1.T, m1[:, :128]))
    top = row == 0
    s_ref[:, 128:] = jnp.where(top, head0[:, 128:], rest[:, 128:])
    normal = jnp.where(top, head0[:, :128], rest[:, :128])
    lower = lax.broadcasted_iota(jnp.int32, (128, 128), 0) >= lax.broadcasted_iota(jnp.int32, (128, 128), 1)
    diagonal = jnp.where(top, dot(head0[:, :128], w0, (1, 1)), dot(rest[:, :128], w1, (1, 1)))
    diagonal = jnp.where(lower, diagonal, 0.0)
    on0 = jnp.where(top, diagonal, low)
    on1 = jnp.where(top, zero, diagonal)
    s_ref[:, :128] = jnp.where(root0, on0, jnp.where(root1, on1, normal))


def cost(flops, size):
    return pl.CostEstimate(flops=flops, bytes_accessed=size, transcendentals=0)


def vmem(count):
    return [pl.BlockSpec(memory_space=pltpu.VMEM)] * count


def factor_corner(whole):
    return pl.pallas_call(
        factor_kernel,
        out_shape=jax.ShapeDtypeStruct((384, 128), F32),
        in_specs=vmem(1),
        out_specs=vmem(1)[0],
        cost_estimate=cost(24 * 10**9, 6 * 2**16),
    )(whole)


def combine(heads, factor, where):
    return pl.pallas_call(
        combine_kernel,
        out_shape=(jax.ShapeDtypeStruct((256, 256), F32), jax.ShapeDtypeStruct((128, 256), F32)),
        grid=(1,),
        in_specs=[pl.BlockSpec(memory_space=pltpu.SMEM), pl.BlockSpec((2, 128, 256), lambda i: (0, 0, 0))] + vmem(1),
        out_specs=tuple(vmem(2)),
        cost_estimate=cost(4 * 10**9, 2**20),
    )(where, heads, factor)


def update_kernel(parts, keys, rows, aliased, place_ref, x_ref, m_ref, s_ref, *refs):
    count = len(parts)
    o_ref, xs, wide, chunk_ref, x_sem, p_sem, o_sem = refs[-7:]
    pieces = refs[: len(refs) - 7 - (1 if aliased else 0)]
    col_z, col_y = place_ref[1] >> 2, place_ref[1] & 3
    for k, (z, y) in enumerate(keys):
        chunk_ref[k] = class_of(col_z + z, col_y + y)

    def rows_of(ref, k):
        return ref.at[pl.ds(pl.multiple_of(chunk_ref[k] * (2 * rows), 2 * rows), 2 * rows)]

    def x_copy(k):
        return pltpu.make_async_copy(rows_of(x_ref, k), xs.at[k], x_sem.at[k])

    def o_copy(k):
        return pltpu.make_async_copy(xs.at[k], rows_of(o_ref, k), o_sem.at[k])

    for k, sources in enumerate(parts):
        x_copy(k).start()
        start = 0
        for which, offset, size in sources:
            for panel in (0, 1):
                pltpu.make_async_copy(
                    pieces[which].at[panel, pl.ds(offset, size)],
                    wide.at[k, pl.ds(start, size), pl.ds(128 * panel, 128)],
                    p_sem.at[k],
                ).start()
            start += size
    m = m_ref[...]
    m_high = m.astype(BF16)
    m_rest = (m - m_high.astype(F32)).astype(BF16)
    m_wide = jnp.concatenate([m_high, m_high, m_rest], axis=0)
    root = place_ref[1] < 2

    def step(k, carry):
        pltpu.make_async_copy(wide.at[k], wide.at[k], p_sem.at[k]).wait()
        value = wide[k]
        high = value.astype(BF16)
        rest = (value - high.astype(F32)).astype(BF16)
        product = jnp.dot(
            jnp.concatenate([high, rest, high], axis=1), m_wide, preferred_element_type=F32
        )
        x_copy(k).wait()
        left = xs[k, pl.ds(0, rows, stride=2), :]
        xs[k, pl.ds(0, rows, stride=2), :] = jnp.where(root, 0.0, left) - product[:, :128]
        xs[k, pl.ds(1, rows, stride=2), :] = xs[k, pl.ds(1, rows, stride=2), :] - product[:, 128:]

        @pl.when((chunk_ref[k] == 0) & (place_ref[0] < 2))
        def _():
            xs[k, pl.ds(0, 128, stride=2), :] = s_ref[:, :128]
            xs[k, pl.ds(1, 128, stride=2), :] = s_ref[:, 128:]

        o_copy(k).start()
        return carry

    lax.fori_loop(0, count, step, 0)

    def finish(k, carry):
        o_copy(k).wait()
        return carry

    lax.fori_loop(0, count, finish, 0)


def update(x, m, special, parts, keys, where, rows, out=None):
    arrays = []
    for sources in parts:
        for array, _, _ in sources:
            if not any(array is other for other in arrays):
                arrays.append(array)
    place_of = lambda array: [other is array for other in arrays].index(True)
    parts = [tuple((place_of(array), offset, size) for array, offset, size in sources) for sources in parts]
    count = len(parts)
    in_hbm = [pl.BlockSpec(memory_space=pltpu.HBM)]
    operands = [where, x, m, special, *arrays] + ([] if out is None else [out])
    return pl.pallas_call(
        functools.partial(update_kernel, parts, keys, rows, out is not None),
        out_shape=jax.ShapeDtypeStruct(x.shape, F32),
        in_specs=[pl.BlockSpec(memory_space=pltpu.SMEM)]
        + in_hbm
        + vmem(2)
        + [pl.BlockSpec(memory_space=pl.ANY)] * (len(operands) - 4),
        out_specs=in_hbm[0],
        scratch_shapes=[
            pltpu.VMEM((count, 2 * rows, 128), F32),
            pltpu.VMEM((count, rows, 256), F32),
            pltpu.SMEM((count,), jnp.int32),
            pltpu.SemaphoreType.DMA((count,)),
            pltpu.SemaphoreType.DMA((count,)),
            pltpu.SemaphoreType.DMA((count,)),
        ],
        cost_estimate=cost(count * rows * 2**18, count * rows * 3 * 2**10),
        input_output_aliases={} if out is None else {len(operands) - 1: 0},
        compiler_params=pltpu.CompilerParams(vmem_limit_bytes=60 * 1024 * 1024),
    )(*operands)


def body(slab):
    row, col = lax.axis_index("row"), lax.axis_index("col")
    x = slab.reshape(slab.shape[0] * 128 * 2, 128)
    rows = x.shape[0] // (2 * PIECES)
    half = rows // 2
    where = jnp.stack([row, col]).astype(jnp.int32)
    top, x = tie(x[:256].reshape(128, 256), x)
    send = Sender(5)
    got = to_workers(send, top[:, :128], row)
    own = extract(x, where, rows)
    heads = lax.all_gather(top, "row", axis=0)
    mine, factor = scatter(send, own, got, row, col)

    send = Sender(99)
    north, south = send(mine, shift(1, 0)), send(mine, shift(-1, 0))
    east, west = send(mine, shift(0, 1)), send(mine, shift(0, -1))
    north, south, east, west = north[0], south[0], east[0], west[0]
    north2, south2 = send(north, shift(1, 0)), send(south, shift(-1, 0))
    factor = share_far(send, factor)
    east2 = send(jnp.concatenate([north, south, east[:, :half]], axis=1), shift(0, 1))
    west2 = send(jnp.concatenate([north, south, west[:, half:]], axis=1), shift(0, -1))
    factor, north2, south2 = tie(factor, north2[0], south2[0])
    factor = share_near(send, factor, col)
    north3, south3 = send(north2, shift(1, 0)), send(south2, shift(-1, 0))
    m, special = combine(heads, factor, where)
    east2 = east2[0]
    corner0, corner1 = send(east2[:, :rows], shift(1, 0)), send(east2[:, rows : 2 * rows], shift(-1, 0))

    def whole_piece(array):
        return ((array, 0, rows),)

    keys = [(0, 0), (1, 0), (-1, 0), (0, 1), (0, -1), (2, 0), (-2, 0), (1, 1), (-1, 1)]
    parts = [whole_piece(v) for v in (mine, north, south, east, west, north2, south2)]
    parts += [((east2, k * rows, rows),) for k in (0, 1)]
    out = update(x, m, special, parts, keys, where, rows)
    west2 = west2[0]
    keys = [(1, -1), (-1, -1), (0, 2), (3, 0), (-3, 0), (2, 1), (-2, 1)]
    parts = [((west2, k * rows, rows),) for k in (0, 1)]
    parts += [((east2, 2 * rows, half), (west2, 2 * rows, half))]
    parts += [whole_piece(v[0]) for v in (north3, south3, corner0, corner1)]
    out = update(x, m, special, parts, keys, where, rows, out)
    return out.reshape(slab.shape)


def solution(mesh):
    spec = P(None, "row", None, None, "col", None)
    return jax.shard_map(body, mesh=mesh, in_specs=(spec,), out_specs=spec, check_vma=False)
```

```python
import functools

import jax
import jax.numpy as jnp
import numpy as np
from jax import lax
from jax.experimental import pallas as pl
from jax.experimental.pallas import tpu as pltpu
from jax.sharding import PartitionSpec as P

F32 = jnp.float32
BF16 = jnp.bfloat16
NZ, NY = 8, 4
ROWS = 8
ROOTS = (0, 1)
SUBROOTS = ((0, 0), (0, 3), (2, 0), (6, 0))
QUARTERS = ((0, 0), (0, 2), (2, 1), (2, 3), (0, 1), (0, 3), (1, 3), (3, 0), (1, 1), (1, 2), (2, 0), (3, 3), (1, 0), (2, 2), (3, 1), (3, 2))
DELIVER = (
    ((0, 9, 2, 0), (1, 10, 3, 1), (2, 16, 1, 1), (3, 19, 0, 0), (8, 15, 3, 0), (9, 28, 3, 1), (24, 13, 2, 0), (25, 29, 3, 1)),
    ((0, 27, 2, 0), (1, 24, 3, 1), (2, 31, 3, 1), (3, 17, 1, 0), (8, 6, 1, 0), (9, 4, 0, 1), (24, 14, 3, 0), (25, 12, 2, 1)),
    ((0, 25, 3, 0), (1, 26, 2, 1), (2, 0, 0, 1), (3, 1, 0, 0), (8, 23, 0, 0), (9, 22, 0, 1), (24, 10, 1, 0), (25, 11, 1, 1)),
    ((0, 2, 1, 0), (1, 8, 2, 1), (2, 6, 2, 1), (3, 30, 3, 0), (8, 26, 2, 0), (9, 14, 3, 1), (24, 28, 3, 0), (25, 5, 0, 1)),
    ((0, 11, 3, 0), (1, 17, 1, 1), (2, 18, 0, 1), (3, 21, 2, 0), (8, 5, 0, 0), (9, 27, 2, 1), (24, 4, 0, 0), (25, 15, 3, 1)),
    ((0, 16, 1, 0), (1, 3, 1, 1), (2, 20, 2, 1), (3, 12, 3, 0), (8, 29, 3, 0), (9, 7, 1, 1), (24, 31, 2, 0), (25, 23, 0, 1)),
    ((0, 18, 0, 0), (1, 19, 0, 1), (2, 13, 3, 1), (3, 7, 2, 0), (8, 20, 1, 0), (9, 21, 1, 1), (24, 22, 0, 0), (25, 30, 2, 1)),
)


WORKERS = (20, 21)


def at(z, y):
    return (z % NZ) * NY + y % NY


def seen_from(root, z, y):
    return at(z, y) if root == 0 else at(z, ROOTS[1] - y)


def place(chip):
    return chip // NY, chip % NY


PIECES = 16
CHIPS = NZ * NY


def class_of(z, y):
    z, y = z & (NZ - 1), y & (NY - 1)
    return (z & 3) * 4 + ((y + ((z >> 2) << 1)) & 3)


def is_in(chips, chip):
    return ((jnp.uint32(sum(1 << c for c in chips)) >> chip.astype(jnp.uint32)) & 1) == 1


def lookup(slots, chip):
    low = is_in([c for c, slot in slots.items() if slot & 1], chip).astype(jnp.int32)
    high = is_in([c for c, slot in slots.items() if slot & 2], chip).astype(jnp.int32)
    return low + 2 * high


def extract_kernel(rows, where_ref, x_ref, *refs):
    outs, buffer, sem = refs[:-2], refs[-2], refs[-1]
    copies = []
    second = where_ref[1] == ROOTS[1]
    for k, (z, y) in enumerate(QUARTERS):
        piece = jnp.where(second, class_of(z, ROOTS[1] - y), class_of(z, y))
        start = pl.multiple_of(piece * (2 * rows), 2 * rows)
        copies.append(pltpu.make_async_copy(x_ref.at[pl.ds(start, 2 * rows)], buffer.at[k], sem.at[k]))
        copies[-1].start()
    for k, copy in enumerate(copies):
        copy.wait()
        outs[k // 4][k % 4] = buffer[k, pl.ds(0, rows, stride=2), :]


def extract(x, where, rows):
    return pl.pallas_call(
        functools.partial(extract_kernel, rows),
        out_shape=(jax.ShapeDtypeStruct((4, rows, 128), F32),) * 4,
        in_specs=[pl.BlockSpec(memory_space=pltpu.SMEM), pl.BlockSpec(memory_space=pltpu.HBM)],
        out_specs=tuple(vmem(4)),
        cost_estimate=cost(0, PIECES * rows * 3 * 2**9),
        scratch_shapes=[pltpu.VMEM((PIECES, 2 * rows, 128), F32), pltpu.SemaphoreType.DMA((PIECES,))],
        compiler_params=pltpu.CompilerParams(vmem_limit_bytes=60 * 1024 * 1024),
    )(where, x)


class Sender:
    def __init__(self, depth):
        self.depth = depth
        self.sent = []

    def __call__(self, value, pairs, axis="col"):
        if len(self.sent) >= self.depth:
            oldest = self.sent[-self.depth]
            value, oldest[0] = lax.optimization_barrier((value, oldest[0]))
        result = [lax.ppermute(value, axis, pairs)]
        self.sent.append(result)
        return result


def tie(*values):
    return lax.optimization_barrier(values)


def shift(fz, fy):
    return [(at(z + fz, y + fy), at(z, y)) for z in range(NZ) for y in range(NY)]


BOTH = ("col", "row")


def cores(pairs, shift=0):
    return [(a * ROWS + i, b * ROWS + 2 * shift + i) for a, b in pairs for i in (0, 1)]


def to_workers(send, block, row):
    swap = [(root * ROWS + i, root * ROWS + 1 - i) for root in ROOTS for i in (0, 1)]
    other = send(block, swap, BOTH)[0]
    pair = jnp.where(row == 0, jnp.concatenate([block, other]), jnp.concatenate([other, block]))
    return send(pair, cores(zip(ROOTS, WORKERS)), BOTH)


def scatter(send, own, got, row, chip):
    quarters = [
        send(own[k], [(root, seen_from(p, *SUBROOTS[k])) for p, root in enumerate(ROOTS)]) for k in (1, 2, 3)
    ]
    got = got[0]
    other = send(got, cores([WORKERS, WORKERS[::-1]]), BOTH)[0]
    quarter = jnp.where(chip < 2, own[0], sum(q[0] for q in quarters))
    arrived = []

    def deal(count):
        for _ in range(count):
            sends = DELIVER[len(arrived)]
            slot = lookup({source: slot for source, _, slot, _ in sends}, chip)
            value = lax.dynamic_index_in_dim(quarter, slot, 0, keepdims=False)
            arrived.append(send(value, [(source, target) for source, target, _, _ in sends]))

    deal(4)
    first, second = jnp.where(chip == WORKERS[0], got, other), jnp.where(chip == WORKERS[0], other, got)
    whole = jnp.concatenate([first, second[128:]])
    factor = lax.cond(is_in(WORKERS, chip) & (row < 2), factor_corner, jnp.zeros_like, whole)
    factor, quarter = tie(factor, quarter)
    deal(1)
    factor = factor + sum(send(factor, cores([(w, w) for w in WORKERS], k), BOTH)[0] for k in (1, 3, 2))
    deal(len(DELIVER) - len(arrived))
    places = {}
    for panel in (0, 1):
        for k, (pz, py) in enumerate(SUBROOTS):
            kinds = [class_of(*m) for m in QUARTERS[4 * k : 4 * k + 4]]
            places[seen_from(panel, pz, py)] = kinds.index(class_of(pz, py))
    held = lax.dynamic_index_in_dim(quarter, lookup(places, chip), 0, keepdims=False)
    mine = []
    for panel in (0, 1):
        value = held
        for k, sends in enumerate(DELIVER):
            got = is_in([target for _, target, _, p in sends if p == panel], chip)
            value = jnp.where(got, arrived[k][0], value)
        mine.append(value)
    return jnp.stack(mine), factor


def share_far(send, factor):
    z, y = place(WORKERS[0])
    line = send(factor, [(at(z, y), at(z, y - 1)), (at(z, y + 1), at(z, y + 2))])[0]
    line = factor + line
    far = send(line, [(at(z, j), at(z + 3, j)) for j in range(NY)])
    back = send(line, [(at(z, j), at(z - 3, j)) for j in range(NY)])
    return line + far[0] + back[0]


def share_near(send, base, chip):
    z = place(WORKERS[0])[0]
    above = send(base, [(at(z + k, j), at(z + k + 1, j)) for k in (0, 3, -3) for j in range(NY)])
    below = send(base, [(at(z + k, j), at(z + k - 1, j)) for k in (0, 3) for j in range(NY)])
    return base + above[0] + below[0]


def dot(a, b, dims):
    return lax.dot_general(
        a, b, ((dims[:1], dims[1:]), ((), ())), precision=lax.Precision.HIGHEST, preferred_element_type=F32
    )


def eliminate(block):
    n = block.shape[0]
    block = 0.5 * (block + block.T)
    row_id = lax.broadcasted_iota(jnp.int32, (8, n), 0)
    lane_id = lax.broadcasted_iota(jnp.int32, (8, n), 1)
    left = [block[8 * k : 8 * k + 8] for k in range(n // 8)]
    right = [jnp.where(lane_id == row_id + 8 * k, 1.0, 0.0).astype(F32) for k in range(n // 8)]
    spread_rows = lambda v, r: jnp.broadcast_to(v[r : r + 1, :], (8, n))
    spread_lanes = lambda v, j: jnp.broadcast_to(v[:, j : j + 1], (8, n))
    for j in range(0, n, 2):
        k0, r = j // 8, j % 8
        lanes0 = [spread_lanes(left[k], j) for k in range(k0, n // 8)]
        lanes1 = [spread_lanes(left[k], j + 1) for k in range(k0, n // 8)]
        a, b, c = spread_rows(lanes0[0], r), spread_rows(lanes0[0], r + 1), spread_rows(lanes1[0], r + 1)
        over = 1.0 / (a * c - b * b)
        done = []
        for part in (left, right):
            row0, row1 = spread_rows(part[k0], r), spread_rows(part[k0], r + 1)
            u0, u1 = (c * row0 - b * row1) * over, (a * row1 - b * row0) * over
            done.append((row0, row1))
            for k in range(k0, n // 8):
                new = part[k] - (lanes0[k - k0] * u0 + lanes1[k - k0] * u1)
                part[k] = jnp.where(row_id > r + 1, new, part[k]) if k == k0 else new
        first = 1.0 / jnp.sqrt(a)
        ratio = b / a
        second = 1.0 / jnp.sqrt(c - b * ratio)
        row0, row1 = done[1]
        right[k0] = jnp.where(
            row_id == r, row0 * first, jnp.where(row_id == r + 1, (row1 - ratio * row0) * second, right[k0])
        )
    return jnp.concatenate(right, axis=0)


def factor_kernel(a_ref, o_ref):
    inverse = eliminate(a_ref[:128])
    o_ref[:128] = inverse
    low = dot(a_ref[128:256], inverse, (1, 1))
    o_ref[128:256] = low
    o_ref[256:] = eliminate(a_ref[256:] - dot(low, low, (1, 1)))


def combine_kernel(place_ref, head_ref, f_ref, m_ref, s_ref):
    row, col = place_ref[0], place_ref[1]
    w0, low, w1 = f_ref[:128], f_ref[128:256], f_ref[256:]
    head0, head1 = head_ref[0], head_ref[1]
    g0 = dot(w0, head0, (1, 0))
    rest = head1 - dot(low, g0, (1, 0))
    g1 = dot(w1, rest, (1, 0))
    m1 = dot(w1, g1, (0, 0))
    m0 = dot(w0, g0 - dot(low, m1, (0, 0)), (0, 0))
    mixed = dot(w0, dot(low, w1, (0, 1)), (0, 0))
    zero = jnp.zeros((128, 128), F32)
    root0, root1 = col == ROOTS[0], col == ROOTS[1]
    m_ref[:128, 128:] = m0[:, 128:]
    m_ref[128:, 128:] = m1[:, 128:]
    m_ref[:128, :128] = jnp.where(root0, -w0.T, jnp.where(root1, mixed, m0[:, :128]))
    m_ref[128:, :128] = jnp.where(root0, zero, jnp.where(root1, -w1.T, m1[:, :128]))
    top = row == 0
    s_ref[:, 128:] = jnp.where(top, head0[:, 128:], rest[:, 128:])
    normal = jnp.where(top, head0[:, :128], rest[:, :128])
    lower = lax.broadcasted_iota(jnp.int32, (128, 128), 0) >= lax.broadcasted_iota(jnp.int32, (128, 128), 1)
    diagonal = jnp.where(top, dot(head0[:, :128], w0, (1, 1)), dot(rest[:, :128], w1, (1, 1)))
    diagonal = jnp.where(lower, diagonal, 0.0)
    on0 = jnp.where(top, diagonal, low)
    on1 = jnp.where(top, zero, diagonal)
    s_ref[:, :128] = jnp.where(root0, on0, jnp.where(root1, on1, normal))


def cost(flops, size):
    return pl.CostEstimate(flops=flops, bytes_accessed=size, transcendentals=0)


def vmem(count):
    return [pl.BlockSpec(memory_space=pltpu.VMEM)] * count


def factor_corner(whole):
    return pl.pallas_call(
        factor_kernel,
        out_shape=jax.ShapeDtypeStruct((384, 128), F32),
        in_specs=vmem(1),
        out_specs=vmem(1)[0],
        cost_estimate=cost(24 * 10**9, 6 * 2**16),
    )(whole)


def combine(heads, factor, where):
    return pl.pallas_call(
        combine_kernel,
        out_shape=(jax.ShapeDtypeStruct((256, 256), F32), jax.ShapeDtypeStruct((128, 256), F32)),
        grid=(1,),
        in_specs=[pl.BlockSpec(memory_space=pltpu.SMEM), pl.BlockSpec((2, 128, 256), lambda i: (0, 0, 0))] + vmem(1),
        out_specs=tuple(vmem(2)),
        cost_estimate=cost(4 * 10**9, 2**20),
    )(where, heads, factor)


def update_kernel(parts, keys, rows, aliased, place_ref, x_ref, m_ref, s_ref, *refs):
    count = len(parts)
    o_ref, xs, wide, chunk_ref, x_sem, p_sem, o_sem = refs[-7:]
    pieces = refs[: len(refs) - 7 - (1 if aliased else 0)]
    col_z, col_y = place_ref[1] >> 2, place_ref[1] & 3
    for k, (z, y) in enumerate(keys):
        chunk_ref[k] = class_of(col_z + z, col_y + y)

    def rows_of(ref, k):
        return ref.at[pl.ds(pl.multiple_of(chunk_ref[k] * (2 * rows), 2 * rows), 2 * rows)]

    def x_copy(k):
        return pltpu.make_async_copy(rows_of(x_ref, k), xs.at[k], x_sem.at[k])

    def o_copy(k):
        return pltpu.make_async_copy(xs.at[k], rows_of(o_ref, k), o_sem.at[k])

    def fetch(k):
        x_copy(k).start()
        start = 0
        for which, offset, size in parts[k]:
            for panel in (0, 1):
                pltpu.make_async_copy(
                    pieces[which].at[panel, pl.ds(offset, size)],
                    wide.at[k, pl.ds(start, size), pl.ds(128 * panel, 128)],
                    p_sem.at[k],
                ).start()
            start += size

    for k in range(min(4, count)):
        fetch(k)
    m = m_ref[...]
    m_high = m.astype(BF16)
    m_rest = (m - m_high.astype(F32)).astype(BF16)
    m_wide = jnp.concatenate([m_high, m_high, m_rest], axis=0)
    root = place_ref[1] < 2

    def step(k, carry):
        pltpu.make_async_copy(wide.at[k], wide.at[k], p_sem.at[k]).wait()
        value = wide[k]
        high = value.astype(BF16)
        rest = (value - high.astype(F32)).astype(BF16)
        product = jnp.dot(
            jnp.concatenate([high, rest, high], axis=1), m_wide, preferred_element_type=F32
        )
        x_copy(k).wait()
        left = xs[k, pl.ds(0, rows, stride=2), :]
        xs[k, pl.ds(0, rows, stride=2), :] = jnp.where(root, 0.0, left) - product[:, :128]
        xs[k, pl.ds(1, rows, stride=2), :] = xs[k, pl.ds(1, rows, stride=2), :] - product[:, 128:]

        @pl.when((chunk_ref[k] == 0) & (place_ref[0] < 2))
        def _():
            xs[k, pl.ds(0, 128, stride=2), :] = s_ref[:, :128]
            xs[k, pl.ds(1, 128, stride=2), :] = s_ref[:, 128:]

        o_copy(k).start()
        return carry

    for k in range(count):
        if k + 4 < count:
            fetch(k + 4)
        step(k, 0)

    def finish(k, carry):
        o_copy(k).wait()
        return carry

    lax.fori_loop(0, count, finish, 0)


def update(x, m, special, parts, keys, where, rows, out=None):
    arrays = []
    for sources in parts:
        for array, _, _ in sources:
            if not any(array is other for other in arrays):
                arrays.append(array)
    place_of = lambda array: [other is array for other in arrays].index(True)
    parts = [tuple((place_of(array), offset, size) for array, offset, size in sources) for sources in parts]
    count = len(parts)
    in_hbm = [pl.BlockSpec(memory_space=pltpu.HBM)]
    operands = [where, x, m, special, *arrays] + ([] if out is None else [out])
    return pl.pallas_call(
        functools.partial(update_kernel, parts, keys, rows, out is not None),
        out_shape=jax.ShapeDtypeStruct(x.shape, F32),
        in_specs=[pl.BlockSpec(memory_space=pltpu.SMEM)]
        + in_hbm
        + vmem(2)
        + [pl.BlockSpec(memory_space=pl.ANY)] * (len(operands) - 4),
        out_specs=in_hbm[0],
        scratch_shapes=[
            pltpu.VMEM((count, 2 * rows, 128), F32),
            pltpu.VMEM((count, rows, 256), F32),
            pltpu.SMEM((count,), jnp.int32),
            pltpu.SemaphoreType.DMA((count,)),
            pltpu.SemaphoreType.DMA((count,)),
            pltpu.SemaphoreType.DMA((count,)),
        ],
        cost_estimate=cost(count * rows * 2**18, count * rows * 3 * 2**10),
        input_output_aliases={} if out is None else {len(operands) - 1: 0},
        compiler_params=pltpu.CompilerParams(vmem_limit_bytes=60 * 1024 * 1024),
    )(*operands)


def body(slab):
    row, col = lax.axis_index("row"), lax.axis_index("col")
    x = slab.reshape(slab.shape[0] * 128 * 2, 128)
    rows = x.shape[0] // (2 * PIECES)
    half = rows // 2
    where = jnp.stack([row, col]).astype(jnp.int32)
    top, x = tie(x[:256].reshape(128, 256), x)
    send = Sender(5)
    got = to_workers(send, top[:, :128], row)
    own = extract(x, where, rows)
    heads = lax.all_gather(top, "row", axis=0)
    mine, factor = scatter(send, own, got, row, col)

    send = Sender(99)
    north, south = send(mine, shift(1, 0)), send(mine, shift(-1, 0))
    east, west = send(mine, shift(0, 1)), send(mine, shift(0, -1))
    north, south, east, west = north[0], south[0], east[0], west[0]
    north2, south2 = send(north, shift(1, 0)), send(south, shift(-1, 0))
    factor = share_far(send, factor)
    east2 = send(jnp.concatenate([north, south, east[:, :half]], axis=1), shift(0, 1))
    west2 = send(jnp.concatenate([north, south, west[:, half:]], axis=1), shift(0, -1))
    factor, north2, south2 = tie(factor, north2[0], south2[0])
    factor = share_near(send, factor, col)
    north3, south3 = send(north2, shift(1, 0)), send(south2, shift(-1, 0))
    m, special = combine(heads, factor, where)
    east2 = east2[0]
    corner0, corner1 = send(east2[:, :rows], shift(1, 0)), send(east2[:, rows : 2 * rows], shift(-1, 0))

    def whole_piece(array):
        return ((array, 0, rows),)

    keys = [(0, 0), (1, 0), (-1, 0), (0, 1), (0, -1), (2, 0), (-2, 0), (1, 1), (-1, 1)]
    parts = [whole_piece(v) for v in (mine, north, south, east, west, north2, south2)]
    parts += [((east2, k * rows, rows),) for k in (0, 1)]
    out = update(x, m, special, parts, keys, where, rows)
    west2 = west2[0]
    keys = [(1, -1), (-1, -1), (0, 2), (3, 0), (-3, 0), (2, 1), (-2, 1)]
    parts = [((west2, k * rows, rows),) for k in (0, 1)]
    parts += [((east2, 2 * rows, half), (west2, 2 * rows, half))]
    parts += [whole_piece(v[0]) for v in (north3, south3, corner0, corner1)]
    out = update(x, m, special, parts, keys, where, rows, out)
    return out.reshape(slab.shape)


def solution(mesh):
    spec = P(None, "row", None, None, "col", None)
    return jax.shard_map(body, mesh=mesh, in_specs=(spec,), out_specs=spec, check_vma=False)
```
